256 devices in a mesh: mode: 64 (over x_hi, y, z), atom: 4 (over x_lo, core).
Axes of the slice: x: 4 (x_hi: 2, x_lo: 2; x = x_hi * 2 + x_lo), y: 4, z: 8, core: 2. Of those that a mesh axis runs over, the one named last changes fastest.
Arguments:
- vectors: bfloat16 [15360, 8192], P('atom', 'mode'), may hold values from -0.046875 to 0.046875
- couplings: float32 [4, 3, 3, 3, 5120], P(None, None, None, None, 'atom'), may hold values from -6 to 6, as said below
- neighbours: int32 [4, 5120], P(None, 'atom'), may hold values from 0 to 5119, as said below
- frequency: float32 [8192], replicated, may hold values from 1 to 2, as said below
Outputs:
- diffusivity: float32 [8192], P('mode')
The draws below stay inside these ranges and needn't reach their ends.
Inputs may be any that keep to these rules, and one draw needn't show every extreme that they name: neighbours[k, i] differs from i by 2 to 64 positions in atom order, counted around the end, upward for k < 2 and downward otherwise; the lists are mutual: neighbours[k + 2, neighbours[k, i]] = i for k < 2; some atoms in every slab have a neighbour exactly 64 positions above and some exactly 64 below. Antisymmetric bonds: couplings[k + 2, a, q, p, j] = -couplings[k, a, p, q, neighbours[k + 2, j]] for k < 2. `frequency`: strictly ascending.
All inputs are finite; a program needn't handle non-finite values.
Results may differ from the reference program's by a relative error of at most 0.00075.
Values may be sent and summed in bfloat16 or wider, within the bound.
No kernel may reach another device: no remote copies, remote signals or barrier semaphores. Data moves between devices by JAX's collectives and lax.ppermute only.
A program may use at most 128 MiB of HBM per device.

```python
import math
import jax
import jax.numpy as jnp
from jax import lax

MODE_DEV = 128
ATOM_DEV = 1280
NEIGHBOURS = 4
HALO = 64
PARTNERS = 4
WIDTH_MODES = 320
BAND = 8192
ATOMS = 5120


def bond_table(key):
    half = NEIGHBOURS // 2
    window = HALO // 2
    offset_base = HALO - window + 1
    windows_all = ATOMS // window
    per_slab = ATOM_DEV // window
    atom_ids = jnp.arange(ATOMS, dtype=jnp.int32)
    window_ids = jnp.arange(windows_all, dtype=jnp.int32)[:, None]
    inner_ids = jnp.arange(window, dtype=jnp.int32)[None, :]
    upward_list = []
    downward_list = []
    for slot in range(half):
        scores = jax.random.randint(jax.random.fold_in(key, 31 + slot), (windows_all, window), 0, 1 << 20) * window + inner_ids
        forced = (window_ids % per_slab == 0) & (inner_ids == 0)
        scores = jnp.where(forced, (1 << 20) * window + window, scores).astype(jnp.int32)
        rank = jnp.argsort(jnp.argsort(scores, axis=1), axis=1).astype(jnp.int32).reshape(ATOMS)
        upward = jnp.mod(atom_ids + offset_base + rank - jnp.mod(atom_ids, window), ATOMS).astype(jnp.int32)
        downward = jnp.zeros((ATOMS,), jnp.int32).at[upward].set(atom_ids)
        upward_list.append(upward)
        downward_list.append(downward)
    return jnp.stack(upward_list + downward_list).astype(jnp.int32)


def draw_neighbours(key, part):
    return bond_table(key)


def draw_couplings(key, part):
    half = NEIGHBOURS // 2
    table = bond_table(key)
    base = jnp.clip(jax.random.normal(jax.random.fold_in(key, 41), (half, 3, 3, 3, ATOMS), jnp.float32), -6.0, 6.0)
    mirrored = []
    for slot in range(half):
        taken = jnp.take(base[slot], table[half + slot], axis=3)
        mirrored.append(-jnp.transpose(taken, (0, 2, 1, 3)))
    return jnp.concatenate([base, jnp.stack(mirrored)], axis=0).astype(jnp.float32)


def draw_frequency(key, part):
    gaps = jnp.exp(jax.random.uniform(jax.random.fold_in(key, 22), (BAND,), jnp.float32, jnp.log(0.25), 0.0))
    total = jnp.sum(gaps)
    position = (jnp.cumsum(gaps) - 0.5 * gaps) / total
    return (1.0 + position).astype(jnp.float32)


def shard_levels(key, shape, cuts, low, high):
    def one(axis_at, shards_of):
        steps = jax.random.uniform(jax.random.fold_in(jax.random.fold_in(key, 6), axis_at), (shards_of,), jnp.float32, low / len(cuts), high / len(cuts))
        return jnp.repeat(jnp.exp(steps), shape[axis_at] // shards_of).reshape((-1,) + (1,) * (len(shape) - axis_at - 1))

    gain = one(*cuts[0])
    for cut in cuts[1:]:
        gain = gain * one(*cut)
    return gain


def scatter_about(own_key, shape, scale, reach, split=(), held_as=jnp.bfloat16):
    level = shard_levels(own_key, shape, split, -0.22, 0.18) if split else 1.0
    drawn = jax.random.normal(own_key, shape, jnp.float32) * scale * level
    return jnp.minimum(jnp.maximum(drawn, -reach), reach).astype(held_as)


def setup_inputs(seed: int = 0) -> dict:
    keys = jax.random.split(jax.random.key(seed), 5)
    return {
        "vectors": scatter_about(keys[0], (3 * ATOMS, BAND), (3 * ATOMS) ** -0.5, 0.046875, ((0, 4), (1, 64))),
        "couplings": draw_couplings(jax.random.fold_in(keys[4], 71), 0),
        "neighbours": draw_neighbours(jax.random.fold_in(keys[4], 71), 0),
        "frequency": draw_frequency(jax.random.fold_in(keys[4], 71), 0),
    }


def velocity(padded, local_index, couplings):
    count = local_index.shape[1]
    block_width = padded.shape[2]
    coupled = jnp.transpose(couplings, (4, 0, 1, 2, 3))
    summed = jnp.zeros((count, 3, 3, block_width), jnp.float32)
    for slot in range(local_index.shape[0]):
        picked = jnp.take(padded, local_index[slot], axis=0).astype(jnp.float32)
        summed = summed + jnp.einsum("iapq,iqm->ipam", coupled[:, slot], picked)
    return summed.astype(jnp.bfloat16).reshape(count * 3, 3 * block_width)


def lorentz(offset, half_width):
    return (half_width / math.pi) / (offset * offset + half_width * half_width)


def weighted(cross_part, row_freq, col_freq, half_width):
    reshaped = cross_part.reshape(cross_part.shape[0], 3, -1)
    squares = jnp.sum(reshaped * reshaped, axis=1)
    return jnp.sum(squares * lorentz(row_freq[:, None] - col_freq[None, :], half_width), axis=1)


def reference(vectors, couplings, neighbours, frequency):
    blocks_all = BAND // MODE_DEV
    half_width = WIDTH_MODES / BAND
    rows_all = 3 * ATOMS
    stacked = vectors.reshape(ATOMS, 3, blocks_all, MODE_DEV).transpose(2, 0, 1, 3)
    applied = lax.map(lambda block_vectors: velocity(block_vectors, neighbours, couplings), stacked)
    flat = stacked.reshape(blocks_all, rows_all, MODE_DEV)
    vec_pad = jnp.concatenate([flat, jnp.zeros((PARTNERS, rows_all, MODE_DEV), flat.dtype)])
    app_pad = jnp.concatenate([applied, jnp.zeros((PARTNERS, rows_all, 3 * MODE_DEV), applied.dtype)])
    freq_pad = jnp.concatenate([frequency, jnp.ones((PARTNERS * MODE_DEV,), frequency.dtype)]).reshape(blocks_all + PARTNERS, MODE_DEV)

    def per_block(block_index):
        own_vec = lax.dynamic_index_in_dim(vec_pad, block_index, 0, keepdims=False)
        own_app = lax.dynamic_index_in_dim(app_pad, block_index, 0, keepdims=False)
        own_freq = lax.dynamic_index_in_dim(freq_pad, block_index, 0, keepdims=False)
        own_sum = weighted(jnp.dot(own_vec.T, own_app, preferred_element_type=jnp.float32), own_freq, own_freq, half_width)
        partner_list = []
        for distance in range(1, PARTNERS + 1):
            far_vec = lax.dynamic_index_in_dim(vec_pad, block_index + distance, 0, keepdims=False)
            far_app = lax.dynamic_index_in_dim(app_pad, block_index + distance, 0, keepdims=False)
            far_freq = lax.dynamic_index_in_dim(freq_pad, block_index + distance, 0, keepdims=False)
            own_sum = own_sum + weighted(jnp.dot(own_vec.T, far_app, preferred_element_type=jnp.float32), own_freq, far_freq, half_width)
            partner_list.append(weighted(jnp.dot(far_vec.T, own_app, preferred_element_type=jnp.float32), far_freq, own_freq, half_width))
        return own_sum, jnp.stack(partner_list)

    own_all, partner_all = lax.map(per_block, jnp.arange(blocks_all, dtype=jnp.int32))
    partner_pad = jnp.concatenate([jnp.zeros((PARTNERS, PARTNERS, MODE_DEV), jnp.float32), partner_all])
    for distance in range(1, PARTNERS + 1):
        own_all = own_all + partner_pad[PARTNERS - distance:PARTNERS - distance + blocks_all, distance - 1]
    freq_own = frequency.reshape(blocks_all, MODE_DEV)
    return (math.pi / (3.0 * freq_own * freq_own) * own_all).reshape(BAND)
```

```python
import functools
import math

import jax
import jax.numpy as jnp
from jax import lax
from jax.experimental import pallas as pl
from jax.experimental.pallas import tpu as pltpu
from jax.sharding import PartitionSpec as P

HALO = 64
PARTNERS = 4
WIDTH_MODES = 320
BLOCK = 128
WIN = BLOCK + 2 * HALO
ROWS = 3 * BLOCK
SPLIT = 7
SLOTS = 5
F32, BF16 = jnp.float32, jnp.bfloat16


def shifted(x, axis, distance):
    count = lax.axis_size(axis)
    return lax.ppermute(x, axis, [(i, (i + distance) % count) for i in range(count)])


def operator_kernel(packed_ref, out_ref, plane_ref):
    lane = lax.broadcasted_iota(jnp.int32, (BLOCK, ROWS), 1)
    atom = lax.broadcasted_iota(jnp.int32, (BLOCK, ROWS), 0)
    spread = jnp.zeros((40, ROWS), F32)
    for p in range(3):
        place = jnp.where(lane == 3 * atom + p, 1.0, 0.0).astype(BF16)
        spread += jnp.dot(packed_ref[p].astype(BF16), place, preferred_element_type=F32)
    target = [spread[36 + k : 37 + k] for k in range(4)]
    same = [target[0] == target[1], target[2] == target[3]]

    def mask(k, first, rows):
        row = lax.broadcasted_iota(jnp.int32, (rows, ROWS), 0).astype(F32) + float(first)
        return row == target[k]

    strips = [(0, HALO, (2, 3)), (HALO, HALO, (0, 1, 2, 3)), (2 * HALO, HALO, (0, 1, 2, 3)), (3 * HALO, HALO, (0, 1))]
    for first, rows, slots in strips:
        masks = {k: mask(k, first, rows) for k in slots}
        for a in range(3):
            for q in range(3):
                value = jnp.zeros((rows, ROWS), F32)
                for k in reversed(slots):
                    at = (k * 3 + a) * 3 + q
                    own = spread[at : at + 1]
                    if k % 2 == 0:
                        twin = spread[at + 9 : at + 10]
                        own = own + jnp.where(same[k // 2], twin, 0.0)
                    value = jnp.where(masks[k], own, value)
                for c in range(3):
                    plane_ref[a, c, pl.ds(3 * first + q, rows, stride=3), :] = value[:, c * 128 : (c + 1) * 128]
    for a in range(3):
        for c in range(3):
            out_ref[0, a, :, c * 128 : (c + 1) * 128] = plane_ref[a, c].astype(BF16)


def build_operator(packed):
    blocks = packed.shape[2] // BLOCK
    return pl.pallas_call(
        operator_kernel,
        grid=(blocks,),
        in_specs=[pl.BlockSpec((3, 40, BLOCK), lambda i: (0, 0, i))],
        out_specs=pl.BlockSpec((1, 3, 3 * WIN, ROWS), lambda i: (i, 0, 0, 0)),
        out_shape=jax.ShapeDtypeStruct((blocks, 3, 3 * WIN, ROWS), BF16),
        scratch_shapes=[pltpu.VMEM((3, 3, 3 * WIN, 128), F32)],
        compiler_params=pltpu.CompilerParams(vmem_limit_bytes=24 * 2**20),
        cost_estimate=pl.CostEstimate(flops=10**9, bytes_accessed=20 * 10**6, transcendentals=0),
    )(packed)


def star_step(window, operator_ref, partners, total_ref):
    window = window.T
    applied = [
        jnp.dot(window, operator_ref[0, a], preferred_element_type=F32).astype(BF16) for a in range(3)
    ]
    applied = jnp.concatenate(applied, axis=0)
    total_ref[...] += jnp.dot(applied, jnp.concatenate(partners, axis=1), preferred_element_type=F32)


def first_kernel(t_ref, far_ref, p0, p1, p2, p3, p4, out_ref):
    g = pl.program_id(0)

    @pl.when(g == 0)
    def _():
        out_ref[...] = jnp.zeros_like(out_ref)

    start = pl.multiple_of((g + 1) * ROWS - 3 * HALO, 3 * HALO)
    window = far_ref[pl.ds(start, 3 * WIN), :]
    star_step(window, t_ref, [r[...] for r in (p0, p1, p2, p3, p4)], out_ref)


def second_kernel(head, t_ref, before_ref, far_a, far_b, own, a0, a1, a2, a3, b0, b1, b2, b3, out_ref, padded, total):
    g = pl.program_id(0)
    steps = pl.num_programs(0)
    edge = 3 * HALO

    @pl.when(g == 0)
    def _():
        rows_a = far_a.shape[0]
        rows_b = far_b.shape[0] - 2 * edge
        padded[0:edge, :] = far_b[rows_b : rows_b + edge, :]
        padded[edge : edge + rows_a, :] = far_a[...]
        padded[edge + rows_a : edge + rows_a + rows_b, :] = far_b[0:rows_b, :]
        padded[edge + rows_a + rows_b :, :] = far_b[rows_b + edge :, :]
        total[...] = before_ref[...]

    block = lax.rem(g + head, head + steps - 1)
    start = pl.multiple_of(block * ROWS, ROWS)
    window = padded[pl.ds(start, 3 * WIN), :]
    in_first = jnp.logical_or(g == 0, g == steps - 1)

    @pl.when(in_first)
    def _():
        star_step(window, t_ref, [a0[...], a1[...], own[...], a2[...], a3[...]], total)

    @pl.when(jnp.logical_not(in_first))
    def _():
        star_step(window, t_ref, [b0[...], b1[...], own[...], b2[...], b3[...]], total)

    @pl.when(g == steps - 1)
    def _():
        for s in range(4):
            for a in range(3):
                out_ref[s, a * 32 : (a + 1) * 32, :] = total[a * 128 + s * 32 : a * 128 + (s + 1) * 32, :].astype(BF16)


def star_products(operator, own, firsts, seconds):
    blocks = operator.shape[0]
    width = own.shape[1]
    head = SPLIT - 1
    op_block = (1, 3, 3 * WIN, ROWS)
    shape = (3 * width, SLOTS * width)
    whole = lambda x: pl.BlockSpec(x.shape, lambda g: (0,) * x.ndim)
    ahead = pl.BlockSpec((ROWS, width), lambda g: (g + 1, 0))
    cost = lambda n: pl.CostEstimate(flops=n * 4 * 10**8, bytes_accessed=n * 3 * 10**6, transcendentals=0)
    before = pl.pallas_call(
        first_kernel,
        grid=(SPLIT - 2,),
        in_specs=[pl.BlockSpec(op_block, lambda g: (g + 1, 0, 0, 0)), whole(firsts[0])] + [ahead] * 5,
        out_specs=pl.BlockSpec(shape, lambda g: (0, 0)),
        out_shape=jax.ShapeDtypeStruct(shape, F32),
        compiler_params=pltpu.CompilerParams(vmem_limit_bytes=24 * 2**20),
        cost_estimate=cost(SPLIT - 2),
    )(operator, firsts[0], firsts[0], firsts[1], own, firsts[2], firsts[3])
    steps = blocks - (SPLIT - 2)
    at = lambda g: lax.rem(g + head, blocks)
    in_a = pl.BlockSpec((ROWS, width), lambda g: (jnp.where(g == steps - 1, 0, head), 0))
    in_b = pl.BlockSpec((ROWS, width), lambda g: (jnp.clip(g - 1, 0, steps - 3), 0))
    out_shape = (4, shape[0] // 4, shape[1])
    return pl.pallas_call(
        functools.partial(second_kernel, head),
        grid=(steps,),
        in_specs=[
            pl.BlockSpec(op_block, lambda g: (at(g), 0, 0, 0)),
            pl.BlockSpec(shape, lambda g: (0, 0)),
            whole(firsts[0]),
            whole(seconds[0]),
            pl.BlockSpec((ROWS, width), lambda g: (at(g), 0)),
        ]
        + [in_a] * 4
        + [in_b] * 4,
        out_specs=pl.BlockSpec(out_shape, lambda g: (0, 0, 0)),
        out_shape=jax.ShapeDtypeStruct(out_shape, BF16),
        scratch_shapes=[pltpu.VMEM((blocks * ROWS + 6 * HALO, width), BF16), pltpu.VMEM(shape, F32)],
        compiler_params=pltpu.CompilerParams(vmem_limit_bytes=32 * 2**20),
        cost_estimate=cost(steps),
    )(operator, before, firsts[0], seconds[0], own, *firsts, *seconds)


def weigh_kernel(half_width, share_ref, s0, s1, s2, s3, centre_ref, freq_ref, valid_ref, out_ref):
    summed = s0[...].astype(F32) + s1[...].astype(F32) + s2[...].astype(F32) + s3[...].astype(F32)
    squares = summed[0:32] * summed[0:32] + summed[32:64] * summed[32:64] + summed[64:96] * summed[64:96]
    row = lax.broadcasted_iota(jnp.int32, (32, 128), 0) + 32 * share_ref[0]
    lane = lax.broadcasted_iota(jnp.int32, (32, 128), 1)
    centre = jnp.zeros((32, 128), F32)
    out_ref[...] = jnp.zeros_like(out_ref)
    for slot in range(SLOTS):
        part = slice(slot * 128, (slot + 1) * 128)
        offset = centre_ref[...] - freq_ref[0:1, part]
        lorentz = (half_width / math.pi) / (offset * offset + half_width * half_width)
        term = squares[:, part] * lorentz * valid_ref[0:1, part]
        centre += term
        if slot > 0:
            out_ref[slot : slot + 1, :] = jnp.sum(term, axis=0, keepdims=True)
    own = jnp.sum(centre, axis=1, keepdims=True)
    out_ref[0:1, :] = jnp.sum(jnp.where(row == lane, own, 0.0), axis=0, keepdims=True)


def local(vectors, couplings, neighbours, frequency):
    rows_dev, width = vectors.shape
    atoms_dev = rows_dev // 3
    atom_groups = lax.axis_size("atom")
    total_atoms = atoms_dev * atom_groups
    atom_at = lax.axis_index("atom")
    mode_at = lax.axis_index("mode")
    modes = lax.axis_size("mode")
    half_width = WIDTH_MODES / (width * modes)
    edge = 3 * HALO
    cut = SPLIT * ROWS

    below = shifted(vectors[rows_dev - edge :], "atom", 1)
    above = shifted(vectors[:edge], "atom", -1)
    own_a = vectors[:cut]
    own_b = vectors[cut:]
    own_b_far = jnp.concatenate([own_b, below, above], axis=0)
    up1a = shifted(own_a, "mode", -1)
    dn1a = shifted(own_a, "mode", 1)
    up1b = shifted(own_b_far, "mode", -1)
    dn1b = shifted(own_b, "mode", 1)
    up2a = shifted(up1a, "mode", -1)
    dn2a = shifted(dn1a, "mode", 1)
    up2b = shifted(up1b, "mode", -1)
    dn2b = shifted(dn1b, "mode", 1)

    atom_ids = lax.broadcasted_iota(jnp.int32, neighbours.shape, 1)
    block_first = atom_at * atoms_dev + (atom_ids // BLOCK) * BLOCK
    target = jnp.mod(neighbours - block_first + HALO, total_atoms).astype(F32)
    packed = jnp.transpose(couplings, (2, 0, 1, 3, 4)).reshape(3, 36, atoms_dev)
    packed = jnp.concatenate([packed, jnp.broadcast_to(target, (3, 4, atoms_dev))], axis=1)
    operator = build_operator(packed)

    partial = star_products(operator, vectors, [up2a, up1a, dn1a, dn2a], [up2b, up1b, dn1b, dn2b])

    share = lambda k: lax.dynamic_index_in_dim(partial, lax.rem(atom_at + k, atom_groups), 0, keepdims=False)
    shares = [share(0)] + [shifted(share(k), "atom", k) for k in range(1, 4)]

    freq_rows = frequency.reshape(modes, width)
    blocks = [lax.rem(mode_at + d + modes, modes) for d in (2, 1, 0, -1, -2)]
    slot_freqs = [lax.dynamic_index_in_dim(freq_rows, b, 0, keepdims=False) for b in blocks]
    freq_lanes = jnp.broadcast_to(jnp.concatenate(slot_freqs)[None], (8, SLOTS * width))
    valid = jnp.stack([(b <= blocks[0]).astype(F32) for b in blocks])
    valid = jnp.broadcast_to(jnp.repeat(valid, width)[None], (8, SLOTS * width))
    centre = lax.dynamic_slice_in_dim(slot_freqs[0], atom_at * 32, 32)
    centre = jnp.broadcast_to(centre[:, None], (32, width))
    vmem = pl.BlockSpec(memory_space=pltpu.VMEM)
    terms = pl.pallas_call(
        functools.partial(weigh_kernel, half_width),
        in_specs=[pl.BlockSpec(memory_space=pltpu.SMEM)] + [vmem] * 7,
        out_specs=vmem,
        out_shape=jax.ShapeDtypeStruct((8, width), F32),
    )(jnp.reshape(atom_at, (1,)).astype(jnp.int32), *shares, centre, freq_lanes, valid)

    result = terms[2]
    result = result + shifted(terms[0], "mode", 2) + shifted(terms[1], "mode", 1)
    result = result + shifted(terms[3], "mode", -1) + shifted(terms[4], "mode", -2)
    far = [lax.ppermute(result, "atom", [(i, i ^ k) for i in range(4)]) for k in range(1, 4)]
    total = (result + far[0]) + (far[1] + far[2])
    own_freq = slot_freqs[2]
    return math.pi / (3.0 * own_freq * own_freq) * total


def solution(mesh):
    return jax.shard_map(
        local,
        mesh=mesh,
        in_specs=(P("atom", "mode"), P(None, None, None, None, "atom"), P(None, "atom"), P()),
        out_specs=P("mode"),
        check_vma=False,
    )
```

```python
import functools
import math

import jax
import jax.numpy as jnp
from jax import lax
from jax.experimental import pallas as pl
from jax.experimental.pallas import tpu as pltpu
from jax.sharding import PartitionSpec as P

HALO = 64
PARTNERS = 4
WIDTH_MODES = 320
BLOCK = 128
WIN = BLOCK + 2 * HALO
ROWS = 3 * BLOCK
SPLIT = 5
SLOTS = 5
F32, BF16 = jnp.float32, jnp.bfloat16


def shifted(x, axis, distance):
    count = lax.axis_size(axis)
    return lax.ppermute(x, axis, [(i, (i + distance) % count) for i in range(count)])


def operator_kernel(total_atoms, place_ref, couplings_ref, neighbours_ref, out_ref, rows_ref):
    i = pl.program_id(0)
    first = (place_ref[0] * pl.num_programs(0) + i) * BLOCK - HALO
    target = neighbours_ref[...] - first
    target = jnp.where(target < 0, target + total_atoms, target)
    target = jnp.where(target >= total_atoms, target - total_atoms, target).astype(F32)
    lane = lax.broadcasted_iota(jnp.int32, (BLOCK, ROWS), 1)
    atom = lax.broadcasted_iota(jnp.int32, (BLOCK, ROWS), 0)
    spread = jnp.zeros((40, ROWS), F32)
    for p in range(3):
        for k in range(4):
            for a in range(3):
                at = (k * 3 + a) * 3
                rows_ref[at : at + 3, :] = couplings_ref[k, a, p]
        rows_ref[36:40, :] = target
        place = jnp.where(lane == 3 * atom + p, 1.0, 0.0).astype(BF16)
        spread += jnp.dot(rows_ref[...].astype(BF16), place, preferred_element_type=F32)
    reach = [spread[36 + k : 37 + k] for k in range(4)]
    same = [reach[0] == reach[1], reach[2] == reach[3]]
    own = {}
    for k in range(4):
        for at in range(k * 9, k * 9 + 9):
            own[at] = spread[at : at + 1]
            if k % 2 == 0:
                own[at] = own[at] + jnp.where(same[k // 2], spread[at + 9 : at + 10], 0.0)
    for first_row, slots in ((0, (2, 3)), (HALO, (0, 1, 2, 3)), (2 * HALO, (0, 1, 2, 3)), (3 * HALO, (0, 1))):
        row = lax.broadcasted_iota(jnp.int32, (HALO, ROWS), 0).astype(F32) + float(first_row)
        masks = {k: row == reach[k] for k in slots}
        for a in range(3):
            for q in range(3):
                value = jnp.zeros((HALO, ROWS), F32)
                for k in reversed(slots):
                    value = jnp.where(masks[k], own[(k * 3 + a) * 3 + q], value)
                start = q * WIN + first_row
                out_ref[0, a, start : start + HALO, :] = value.astype(BF16)


def build_operator(place, couplings, neighbours, total_atoms):
    blocks = neighbours.shape[1] // BLOCK
    return pl.pallas_call(
        functools.partial(operator_kernel, total_atoms),
        grid=(blocks,),
        in_specs=[
            pl.BlockSpec(memory_space=pltpu.SMEM),
            pl.BlockSpec((4, 3, 3, 3, BLOCK), lambda i: (0, 0, 0, 0, i)),
            pl.BlockSpec((4, BLOCK), lambda i: (0, i)),
        ],
        out_specs=pl.BlockSpec((1, 3, 3 * WIN, ROWS), lambda i: (i, 0, 0, 0)),
        out_shape=jax.ShapeDtypeStruct((blocks, 3, 3 * WIN, ROWS), BF16),
        scratch_shapes=[pltpu.VMEM((40, BLOCK), F32)],
        compiler_params=pltpu.CompilerParams(vmem_limit_bytes=24 * 2**20),
        cost_estimate=pl.CostEstimate(flops=4 * 10**9, bytes_accessed=20 * 10**6, transcendentals=0),
    )(place, couplings, neighbours)


def copy_kernel(moves, *refs):
    sems = refs[-1]
    copies = [
        pltpu.make_async_copy(refs[src].at[pl.ds(s0, n)], refs[dst].at[pl.ds(d0, n)], sems.at[c])
        for c, (src, s0, dst, d0, n) in enumerate(moves)
    ]
    for copy in copies:
        copy.start()
    for copy in copies:
        copy.wait()


def copied_rows(inputs, lengths, moves):
    width = inputs[0].shape[1]
    moves = [(i, s, len(inputs) + o, d, n) for i, s, o, d, n in moves]
    return pl.pallas_call(
        functools.partial(copy_kernel, moves),
        in_specs=[pl.BlockSpec(memory_space=pl.ANY)] * len(inputs),
        out_specs=[pl.BlockSpec(memory_space=pl.ANY)] * len(lengths),
        out_shape=[jax.ShapeDtypeStruct((n, width), inputs[0].dtype) for n in lengths],
        scratch_shapes=[pltpu.SemaphoreType.DMA((len(moves),))],
    )(*inputs)


def star_step(planes_ref, start, operator_ref, partners, total_ref):
    window = [planes_ref[pl.ds(start + q, WIN, stride=3), :].astype(BF16) for q in range(3)]
    window = jnp.concatenate(window, axis=0).T
    applied = [jnp.dot(window, operator_ref[0, a], preferred_element_type=F32).astype(BF16) for a in range(3)]
    applied = jnp.concatenate(applied, axis=0)
    total_ref[...] += jnp.dot(applied, jnp.concatenate(partners, axis=1), preferred_element_type=F32)


def first_kernel(t_ref, far_ref, p0, p1, p2, p3, p4, out_ref, planes):
    g = pl.program_id(0)

    @pl.when(g == 0)
    def _():
        out_ref[...] = jnp.zeros_like(out_ref)
        planes[...] = far_ref[...].astype(F32)

    start = (g + 1) * ROWS - 3 * HALO
    star_step(planes, start, t_ref, [r[...] for r in (p0, p1, p2, p3, p4)], out_ref)


def second_kernel(
    head, place_ref, t_ref, before_ref, far_a, far_b, own, a0, a1, a2, a3, b0, b1, b2, b3, o0, o1, o2, o3, planes, total
):
    g = pl.program_id(0)
    steps = pl.num_programs(0)
    edge = 3 * HALO

    @pl.when(g == 0)
    def _():
        rows_a = far_a.shape[0]
        rows_b = far_b.shape[0] - 2 * edge
        planes[0:edge, :] = far_b[rows_b : rows_b + edge, :].astype(F32)
        planes[edge : edge + rows_a, :] = far_a[...].astype(F32)
        planes[edge + rows_a : edge + rows_a + rows_b, :] = far_b[0:rows_b, :].astype(F32)
        planes[edge + rows_a + rows_b :, :] = far_b[rows_b + edge :, :].astype(F32)
        total[...] = before_ref[...]

    block = lax.rem(g + head, head + steps - 1)
    in_first = jnp.logical_or(g == 0, g == steps - 1)

    @pl.when(in_first)
    def _():
        star_step(planes, block * ROWS, t_ref, [a0[...], a1[...], own[...], a2[...], a3[...]], total)

    @pl.when(jnp.logical_not(in_first))
    def _():
        star_step(planes, block * ROWS, t_ref, [b0[...], b1[...], own[...], b2[...], b3[...]], total)

    @pl.when(g == steps - 1)
    def _():
        for k, out in enumerate((o0, o1, o2, o3)):
            share = jnp.bitwise_xor(place_ref[0], k)
            for a in range(3):
                rows = pl.ds(pl.multiple_of(a * 128 + share * 32, 32), 32)
                out[a * 32 : (a + 1) * 32, :] = total[rows, :].astype(BF16)


def star_products(place, operator, own, firsts, seconds):
    blocks = operator.shape[0]
    width = own.shape[1]
    head = SPLIT - 1
    op_block = (1, 3, 3 * WIN, ROWS)
    shape = (3 * width, SLOTS * width)
    whole = lambda x: pl.BlockSpec(x.shape, lambda g: (0,) * x.ndim)
    ahead = pl.BlockSpec((ROWS, width), lambda g: (g + 1, 0))
    cost = lambda n: pl.CostEstimate(flops=n * 10**9, bytes_accessed=n * 3 * 10**6, transcendentals=0)
    before = pl.pallas_call(
        first_kernel,
        grid=(SPLIT - 2,),
        in_specs=[pl.BlockSpec(op_block, lambda g: (g + 1, 0, 0, 0)), whole(firsts[0])] + [ahead] * 5,
        out_specs=pl.BlockSpec(shape, lambda g: (0, 0)),
        out_shape=jax.ShapeDtypeStruct(shape, F32),
        scratch_shapes=[pltpu.VMEM(firsts[0].shape, F32)],
        compiler_params=pltpu.CompilerParams(vmem_limit_bytes=24 * 2**20),
        cost_estimate=cost(SPLIT - 2),
    )(operator, firsts[0], firsts[0], firsts[1], own, firsts[2], firsts[3])
    steps = blocks - (SPLIT - 2)
    at = lambda g: lax.rem(g + head, blocks)
    in_a = pl.BlockSpec((ROWS, width), lambda g: (jnp.where(g == steps - 1, 0, head), 0))
    in_b = pl.BlockSpec((ROWS, width), lambda g: (jnp.clip(g - 1, 0, steps - 3), 0))
    out_shape = (shape[0] // 4, shape[1])
    return pl.pallas_call(
        functools.partial(second_kernel, head),
        grid=(steps,),
        in_specs=[
            pl.BlockSpec(memory_space=pltpu.SMEM),
            pl.BlockSpec(op_block, lambda g: (at(g), 0, 0, 0)),
            pl.BlockSpec(shape, lambda g: (0, 0)),
            whole(firsts[0]),
            whole(seconds[0]),
            pl.BlockSpec((ROWS, width), lambda g: (at(g), 0)),
        ]
        + [in_a] * 4
        + [in_b] * 4,
        out_specs=[pl.BlockSpec(out_shape, lambda g: (0, 0))] * 4,
        out_shape=[jax.ShapeDtypeStruct(out_shape, BF16)] * 4,
        scratch_shapes=[pltpu.VMEM((blocks * ROWS + 6 * HALO, width), F32), pltpu.VMEM(shape, F32)],
        compiler_params=pltpu.CompilerParams(vmem_limit_bytes=32 * 2**20),
        cost_estimate=cost(steps),
    )(place, operator, before, firsts[0], seconds[0], own, *firsts, *seconds)


RETURNS = (1, -1, 2, -2)


def weigh_kernel(half_width, place_ref, s0, s1, s2, s3, freq_ref, o0, o1, o2, o3, stay_ref, rows_ref):
    atom, mode = place_ref[0], place_ref[1]
    modes = freq_ref.shape[0]
    summed = s0[...].astype(F32) + s1[...].astype(F32) + s2[...].astype(F32) + s3[...].astype(F32)
    squares = summed[0:32] * summed[0:32] + summed[32:64] * summed[32:64] + summed[64:96] * summed[64:96]
    row = lax.broadcasted_iota(jnp.int32, (32, 128), 0) + 32 * atom
    lane = lax.broadcasted_iota(jnp.int32, (32, 128), 1)
    wrapped = lambda b: jnp.where(b >= modes, b - modes, jnp.where(b < 0, b + modes, b))
    top = wrapped(mode + 2)
    top_freq = freq_ref[pl.ds(top, 1), :]
    centre = jnp.sum(jnp.where(row == lane, top_freq, 0.0), axis=1, keepdims=True)
    own = jnp.zeros((32, 128), F32)
    for slot in range(SLOTS):
        block = wrapped(mode + 2 - slot)
        offset = centre - freq_ref[pl.ds(block, 1), :]
        lorentz = (half_width / math.pi) / (offset * offset + half_width * half_width)
        term = jnp.where(block <= top, squares[:, slot * 128 : (slot + 1) * 128] * lorentz, 0.0)
        own += term
        if slot == 2:
            stay_ref[...] = jnp.sum(term, axis=0, keepdims=True)
        elif slot > 0:
            at = RETURNS.index(2 - slot)
            rows_ref[at : at + 1, :] = jnp.sum(term, axis=0, keepdims=True)
    own = jnp.sum(own, axis=1, keepdims=True)
    at = RETURNS.index(2)
    rows_ref[at : at + 1, :] = jnp.sum(jnp.where(row == lane, own, 0.0), axis=0, keepdims=True)
    for k, out in enumerate((o0, o1, o2, o3)):
        out[...] = rows_ref[pl.ds(jnp.bitwise_xor(atom, k), 1), :]


def swapped(x, k):
    return lax.ppermute(x, "atom", [(i, i ^ k) for i in range(4)])


def local(vectors, couplings, neighbours, frequency):
    rows_dev, width = vectors.shape
    atoms_dev = rows_dev // 3
    atom_groups = lax.axis_size("atom")
    modes = lax.axis_size("mode")
    half_width = WIDTH_MODES / (width * modes)
    place = jnp.stack([lax.axis_index("atom"), lax.axis_index("mode")]).astype(jnp.int32)
    edge = 3 * HALO
    cut = SPLIT * ROWS

    own_a, own_b, tail, front = copied_rows(
        [vectors],
        [cut, rows_dev - cut, edge, edge],
        [(0, 0, 0, 0, cut), (0, cut, 1, 0, rows_dev - cut), (0, rows_dev - edge, 2, 0, edge), (0, 0, 3, 0, edge)],
    )
    below = shifted(tail, "atom", 1)
    above = shifted(front, "atom", -1)
    up1a = shifted(own_a, "mode", -1)
    dn1a = shifted(own_a, "mode", 1)
    rest = rows_dev - cut
    [own_b_far] = copied_rows(
        [own_b, below, above],
        [rest + 2 * edge],
        [(0, 0, 0, 0, rest), (1, 0, 0, rest, edge), (2, 0, 0, rest + edge, edge)],
    )
    up1b = shifted(own_b_far, "mode", -1)
    dn1b = shifted(own_b, "mode", 1)
    couplings, own_b_far = lax.optimization_barrier((couplings, own_b_far))
    operator = build_operator(place, couplings, neighbours, atoms_dev * atom_groups)
    up1a, dn1a, operator = lax.optimization_barrier((up1a, dn1a, operator))
    up2a = shifted(up1a, "mode", -1)
    dn2a = shifted(dn1a, "mode", 1)
    up2b = shifted(up1b, "mode", -1)
    dn2b = shifted(dn1b, "mode", 1)

    shares = star_products(place, operator, vectors, [up2a, up1a, dn1a, dn2a], [up2b, up1b, dn1b, dn2b])
    shares = [shares[0]] + [swapped(shares[k], k) for k in range(1, 4)]

    vmem = pl.BlockSpec(memory_space=pltpu.VMEM)
    row = jax.ShapeDtypeStruct((1, width), F32)
    *terms, stay = pl.pallas_call(
        functools.partial(weigh_kernel, half_width),
        in_specs=[pl.BlockSpec(memory_space=pltpu.SMEM)] + [vmem] * 5,
        out_specs=[vmem] * 5,
        out_shape=[row] * 5,
        scratch_shapes=[pltpu.VMEM((4, width), F32)],
    )(place, *shares, frequency.reshape(modes, width))
    carried = terms[0]
    for k in range(1, 4):
        carried = carried + swapped(terms[k], k)
    route = [(b * 4 + s, (b + RETURNS[s]) % modes * 4 + s) for b in range(modes) for s in range(4)]
    result = stay + lax.ppermute(carried, ("mode", "atom"), route)
    far = [swapped(result, k) for k in range(1, 4)]
    total = (result + far[0]) + (far[1] + far[2])
    own_freq = lax.dynamic_slice_in_dim(frequency, place[1] * width, width)
    return math.pi / (3.0 * own_freq * own_freq) * total.reshape(width)


def solution(mesh):
    return jax.shard_map(
        local,
        mesh=mesh,
        in_specs=(P("atom", "mode"), P(None, None, None, None, "atom"), P(None, "atom"), P()),
        out_specs=P("mode"),
        check_vma=False,
    )
```

```python
import functools
import math

import jax
import jax.numpy as jnp
from jax import lax
from jax.experimental import pallas as pl
from jax.experimental.pallas import tpu as pltpu
from jax.sharding import PartitionSpec as P

HALO = 64
PARTNERS = 4
WIDTH_MODES = 320
BLOCK = 128
WIN = BLOCK + 2 * HALO
ROWS = 3 * BLOCK
SPLIT = 5
SLOTS = 5
F32, BF16 = jnp.float32, jnp.bfloat16


def shifted(x, axis, distance):
    count = lax.axis_size(axis)
    return lax.ppermute(x, axis, [(i, (i + distance) % count) for i in range(count)])


def operator_kernel(total_atoms, place_ref, couplings_ref, neighbours_ref, out_ref, rows_ref):
    i = pl.program_id(0)
    first = (place_ref[0] * pl.num_programs(0) + i) * BLOCK - HALO
    target = neighbours_ref[...] - first
    target = jnp.where(target < 0, target + total_atoms, target)
    target = jnp.where(target >= total_atoms, target - total_atoms, target).astype(F32)
    lane = lax.broadcasted_iota(jnp.int32, (BLOCK, ROWS), 1)
    atom = lax.broadcasted_iota(jnp.int32, (BLOCK, ROWS), 0)
    spread = jnp.zeros((40, ROWS), F32)
    for p in range(3):
        for k in range(4):
            for a in range(3):
                at = (k * 3 + a) * 3
                rows_ref[at : at + 3, :] = couplings_ref[k, a, p]
        rows_ref[36:40, :] = target
        place = jnp.where(lane == 3 * atom + p, 1.0, 0.0).astype(BF16)
        spread += jnp.dot(rows_ref[...].astype(BF16), place, preferred_element_type=F32)
    reach = [spread[36 + k : 37 + k] for k in range(4)]
    same = [reach[0] == reach[1], reach[2] == reach[3]]
    own = {}
    for k in range(4):
        for at in range(k * 9, k * 9 + 9):
            own[at] = spread[at : at + 1]
            if k % 2 == 0:
                own[at] = own[at] + jnp.where(same[k // 2], spread[at + 9 : at + 10], 0.0)
    tile = 16
    for c in range(3):
        lanes = slice(c * 128, (c + 1) * 128)
        wide = {at: jnp.broadcast_to(own[at][:, lanes], (tile, 128)) for at in own}
        goal = [jnp.broadcast_to(reach[k][:, lanes], (tile, 128)) for k in range(4)]
        for first_row in range(0, WIN, tile):
            slots = ((2, 3), (0, 1, 2, 3), (0, 1, 2, 3), (0, 1))[first_row // HALO]
            row = lax.broadcasted_iota(jnp.int32, (tile, 128), 0).astype(F32) + float(first_row)
            masks = {k: row == goal[k] for k in slots}
            for a in range(3):
                for q in range(3):
                    value = jnp.zeros((tile, 128), F32)
                    for k in reversed(slots):
                        value = jnp.where(masks[k], wide[(k * 3 + a) * 3 + q], value)
                    start = q * WIN + first_row
                    out_ref[0, a, start : start + tile, lanes] = value.astype(BF16)


def build_operator(place, couplings, neighbours, total_atoms):
    blocks = neighbours.shape[1] // BLOCK
    return pl.pallas_call(
        functools.partial(operator_kernel, total_atoms),
        grid=(blocks,),
        in_specs=[
            pl.BlockSpec(memory_space=pltpu.SMEM),
            pl.BlockSpec((4, 3, 3, 3, BLOCK), lambda i: (0, 0, 0, 0, i)),
            pl.BlockSpec((4, BLOCK), lambda i: (0, i)),
        ],
        out_specs=pl.BlockSpec((1, 3, 3 * WIN, ROWS), lambda i: (i, 0, 0, 0)),
        out_shape=jax.ShapeDtypeStruct((blocks, 3, 3 * WIN, ROWS), BF16),
        scratch_shapes=[pltpu.VMEM((40, BLOCK), F32)],
        compiler_params=pltpu.CompilerParams(vmem_limit_bytes=24 * 2**20),
        cost_estimate=pl.CostEstimate(flops=4 * 10**9, bytes_accessed=20 * 10**6, transcendentals=0),
    )(place, couplings, neighbours)


def copy_kernel(moves, *refs):
    for src, s0, dst, d0, n in moves:
        refs[dst][d0 : d0 + n, :] = refs[src][s0 : s0 + n, :]


def copied_rows(inputs, lengths, moves):
    width = inputs[0].shape[1]
    moves = [(i, s, len(inputs) + o, d, n) for i, s, o, d, n in moves]
    return pl.pallas_call(
        functools.partial(copy_kernel, moves),
        out_shape=[jax.ShapeDtypeStruct((n, width), inputs[0].dtype) for n in lengths],
    )(*inputs)


def star_step(planes_ref, start, operator_ref, partners, total_ref):
    window = [planes_ref[pl.ds(start + q, WIN, stride=3), :].astype(BF16) for q in range(3)]
    window = jnp.concatenate(window, axis=0).T
    applied = [jnp.dot(window, operator_ref[0, a], preferred_element_type=F32).astype(BF16) for a in range(3)]
    applied = jnp.concatenate(applied, axis=0)
    total_ref[...] += jnp.dot(applied, jnp.concatenate(partners, axis=1), preferred_element_type=F32)


def first_kernel(t_ref, far_ref, p0, p1, p2, p3, p4, out_ref, planes):
    g = pl.program_id(0)

    @pl.when(g == 0)
    def _():
        out_ref[...] = jnp.zeros_like(out_ref)
        planes[...] = far_ref[...].astype(F32)

    start = (g + 1) * ROWS - 3 * HALO
    star_step(planes, start, t_ref, [r[...] for r in (p0, p1, p2, p3, p4)], out_ref)


def second_kernel(
    head, place_ref, t_ref, before_ref, far_a, far_b, own, a0, a1, a2, a3, b0, b1, b2, b3, o0, o1, o2, o3, planes, total
):
    g = pl.program_id(0)
    steps = pl.num_programs(0)
    edge = 3 * HALO

    @pl.when(g == 0)
    def _():
        rows_a = far_a.shape[0]
        rows_b = far_b.shape[0] - 2 * edge
        planes[0:edge, :] = far_b[rows_b : rows_b + edge, :].astype(F32)
        planes[edge : edge + rows_a, :] = far_a[...].astype(F32)
        planes[edge + rows_a : edge + rows_a + rows_b, :] = far_b[0:rows_b, :].astype(F32)
        planes[edge + rows_a + rows_b :, :] = far_b[rows_b + edge :, :].astype(F32)
        total[...] = before_ref[...]

    block = lax.rem(g + head, head + steps - 1)
    in_first = jnp.logical_or(g == 0, g == steps - 1)

    @pl.when(in_first)
    def _():
        star_step(planes, block * ROWS, t_ref, [a0[...], a1[...], own[...], a2[...], a3[...]], total)

    @pl.when(jnp.logical_not(in_first))
    def _():
        star_step(planes, block * ROWS, t_ref, [b0[...], b1[...], own[...], b2[...], b3[...]], total)

    @pl.when(g == steps - 1)
    def _():
        for k, out in enumerate((o0, o1, o2, o3)):
            share = jnp.bitwise_xor(place_ref[0], k)
            for a in range(3):
                rows = pl.ds(pl.multiple_of(a * 128 + share * 32, 32), 32)
                out[a * 32 : (a + 1) * 32, :] = total[rows, :].astype(BF16)


def star_products(place, operator, own, firsts, seconds):
    blocks = operator.shape[0]
    width = own.shape[1]
    head = SPLIT - 1
    op_block = (1, 3, 3 * WIN, ROWS)
    shape = (3 * width, SLOTS * width)
    whole = lambda x: pl.BlockSpec(x.shape, lambda g: (0,) * x.ndim)
    ahead = pl.BlockSpec((ROWS, width), lambda g: (g + 1, 0))
    cost = lambda n: pl.CostEstimate(flops=n * 10**9, bytes_accessed=n * 3 * 10**6, transcendentals=0)
    before = pl.pallas_call(
        first_kernel,
        grid=(SPLIT - 2,),
        in_specs=[pl.BlockSpec(op_block, lambda g: (g + 1, 0, 0, 0)), whole(firsts[0])] + [ahead] * 5,
        out_specs=pl.BlockSpec(shape, lambda g: (0, 0)),
        out_shape=jax.ShapeDtypeStruct(shape, F32),
        scratch_shapes=[pltpu.VMEM(firsts[0].shape, F32)],
        compiler_params=pltpu.CompilerParams(vmem_limit_bytes=24 * 2**20),
        cost_estimate=cost(SPLIT - 2),
    )(operator, firsts[0], firsts[0], firsts[1], own, firsts[2], firsts[3])
    steps = blocks - (SPLIT - 2)
    at = lambda g: lax.rem(g + head, blocks)
    in_a = pl.BlockSpec((ROWS, width), lambda g: (jnp.where(g == steps - 1, 0, head), 0))
    in_b = pl.BlockSpec((ROWS, width), lambda g: (jnp.clip(g - 1, 0, steps - 3), 0))
    out_shape = (shape[0] // 4, shape[1])
    return pl.pallas_call(
        functools.partial(second_kernel, head),
        grid=(steps,),
        in_specs=[
            pl.BlockSpec(memory_space=pltpu.SMEM),
            pl.BlockSpec(op_block, lambda g: (at(g), 0, 0, 0)),
            pl.BlockSpec(shape, lambda g: (0, 0)),
            whole(firsts[0]),
            whole(seconds[0]),
            pl.BlockSpec((ROWS, width), lambda g: (at(g), 0)),
        ]
        + [in_a] * 4
        + [in_b] * 4,
        out_specs=[pl.BlockSpec(out_shape, lambda g: (0, 0))] * 4,
        out_shape=[jax.ShapeDtypeStruct(out_shape, BF16)] * 4,
        scratch_shapes=[pltpu.VMEM((blocks * ROWS + 6 * HALO, width), F32), pltpu.VMEM(shape, F32)],
        compiler_params=pltpu.CompilerParams(vmem_limit_bytes=32 * 2**20),
        cost_estimate=cost(steps),
    )(place, operator, before, firsts[0], seconds[0], own, *firsts, *seconds)


RETURNS = (1, -1, 2, -2)


def weigh_kernel(half_width, place_ref, s0, s1, s2, s3, freq_ref, o0, o1, o2, o3, stay_ref, rows_ref):
    atom, mode = place_ref[0], place_ref[1]
    modes = freq_ref.shape[0]
    summed = s0[...].astype(F32) + s1[...].astype(F32) + s2[...].astype(F32) + s3[...].astype(F32)
    squares = summed[0:32] * summed[0:32] + summed[32:64] * summed[32:64] + summed[64:96] * summed[64:96]
    row = lax.broadcasted_iota(jnp.int32, (32, 128), 0) + 32 * atom
    lane = lax.broadcasted_iota(jnp.int32, (32, 128), 1)
    wrapped = lambda b: jnp.where(b >= modes, b - modes, jnp.where(b < 0, b + modes, b))
    top = wrapped(mode + 2)
    top_freq = freq_ref[pl.ds(top, 1), :]
    centre = jnp.sum(jnp.where(row == lane, top_freq, 0.0), axis=1, keepdims=True)
    own = jnp.zeros((32, 128), F32)
    for slot in range(SLOTS):
        block = wrapped(mode + 2 - slot)
        offset = centre - freq_ref[pl.ds(block, 1), :]
        lorentz = (half_width / math.pi) / (offset * offset + half_width * half_width)
        term = jnp.where(block <= top, squares[:, slot * 128 : (slot + 1) * 128] * lorentz, 0.0)
        own += term
        if slot == 2:
            stay_ref[...] = jnp.sum(term, axis=0, keepdims=True)
        elif slot > 0:
            at = RETURNS.index(2 - slot)
            rows_ref[at : at + 1, :] = jnp.sum(term, axis=0, keepdims=True)
    own = jnp.sum(own, axis=1, keepdims=True)
    at = RETURNS.index(2)
    rows_ref[at : at + 1, :] = jnp.sum(jnp.where(row == lane, own, 0.0), axis=0, keepdims=True)
    for k, out in enumerate((o0, o1, o2, o3)):
        out[...] = rows_ref[pl.ds(jnp.bitwise_xor(atom, k), 1), :]


def swapped(x, k):
    return lax.ppermute(x, "atom", [(i, i ^ k) for i in range(4)])


def local(vectors, couplings, neighbours, frequency):
    rows_dev, width = vectors.shape
    atoms_dev = rows_dev // 3
    atom_groups = lax.axis_size("atom")
    modes = lax.axis_size("mode")
    half_width = WIDTH_MODES / (width * modes)
    place = jnp.stack([lax.axis_index("atom"), lax.axis_index("mode")]).astype(jnp.int32)
    edge = 3 * HALO
    cut = SPLIT * ROWS

    own_a, own_b, tail, front = copied_rows(
        [vectors],
        [cut, rows_dev - cut, edge, edge],
        [(0, 0, 0, 0, cut), (0, cut, 1, 0, rows_dev - cut), (0, rows_dev - edge, 2, 0, edge), (0, 0, 3, 0, edge)],
    )
    below = shifted(tail, "atom", 1)
    above = shifted(front, "atom", -1)
    up1a = shifted(own_a, "mode", -1)
    dn1a = shifted(own_a, "mode", 1)
    own_b_far = jnp.concatenate([own_b, below, above], axis=0)
    up1b = shifted(own_b_far, "mode", -1)
    dn1b = shifted(own_b, "mode", 1)
    up2a = shifted(up1a, "mode", -1)
    dn2a = shifted(dn1a, "mode", 1)
    couplings, up1b, dn1b = lax.optimization_barrier((couplings, up1b, dn1b))
    operator = build_operator(place, couplings, neighbours, atoms_dev * atom_groups)
    up2b = shifted(up1b, "mode", -1)
    dn2b = shifted(dn1b, "mode", 1)

    shares = star_products(place, operator, vectors, [up2a, up1a, dn1a, dn2a], [up2b, up1b, dn1b, dn2b])
    shares = [shares[0]] + [swapped(shares[k], k) for k in range(1, 4)]

    vmem = pl.BlockSpec(memory_space=pltpu.VMEM)
    row = jax.ShapeDtypeStruct((1, width), F32)
    *terms, stay = pl.pallas_call(
        functools.partial(weigh_kernel, half_width),
        in_specs=[pl.BlockSpec(memory_space=pltpu.SMEM)] + [vmem] * 5,
        out_specs=[vmem] * 5,
        out_shape=[row] * 5,
        scratch_shapes=[pltpu.VMEM((4, width), F32)],
    )(place, *shares, frequency.reshape(modes, width))
    carried = terms[0]
    for k in range(1, 4):
        carried = carried + swapped(terms[k], k)
    route = [(b * 4 + s, (b + RETURNS[s]) % modes * 4 + s) for b in range(modes) for s in range(4)]
    result = stay + lax.ppermute(carried, ("mode", "atom"), route)
    far = [swapped(result, k) for k in range(1, 4)]
    total = (result + far[0]) + (far[1] + far[2])
    own_freq = lax.dynamic_slice_in_dim(frequency, place[1] * width, width)
    return math.pi / (3.0 * own_freq * own_freq) * total.reshape(width)


def solution(mesh):
    return jax.shard_map(
        local,
        mesh=mesh,
        in_specs=(P("atom", "mode"), P(None, None, None, None, "atom"), P(None, "atom"), P()),
        out_specs=P("mode"),
        check_vma=False,
    )
```

```python
import functools
import math

import jax
import jax.numpy as jnp
from jax import lax
from jax.experimental import pallas as pl
from jax.experimental.pallas import tpu as pltpu
from jax.sharding import PartitionSpec as P

HALO = 64
PARTNERS = 4
WIDTH_MODES = 320
BLOCK = 128
WIN = BLOCK + 2 * HALO
ROWS = 3 * BLOCK
HEAD, TAIL = 2, 3
SLOTS = 5
F32, BF16 = jnp.float32, jnp.bfloat16


def shifted(x, axis, distance):
    count = lax.axis_size(axis)
    return lax.ppermute(x, axis, [(i, (i + distance) % count) for i in range(count)])


def operator_kernel(total_atoms, place_ref, couplings_ref, neighbours_ref, out_ref, rows_ref):
    i = pl.program_id(0)
    first = (place_ref[0] * pl.num_programs(0) + i) * BLOCK - HALO
    target = neighbours_ref[...] - first
    target = jnp.where(target < 0, target + total_atoms, target)
    target = jnp.where(target >= total_atoms, target - total_atoms, target).astype(F32)
    lane = lax.broadcasted_iota(jnp.int32, (BLOCK, ROWS), 1)
    atom = lax.broadcasted_iota(jnp.int32, (BLOCK, ROWS), 0)
    spread = jnp.zeros((40, ROWS), F32)
    for p in range(3):
        for k in range(4):
            for a in range(3):
                at = (k * 3 + a) * 3
                rows_ref[at : at + 3, :] = couplings_ref[k, a, p]
        rows_ref[36:40, :] = target
        place = jnp.where(lane == 3 * atom + p, 1.0, 0.0).astype(BF16)
        spread += jnp.dot(rows_ref[...].astype(BF16), place, preferred_element_type=F32)
    reach = [spread[36 + k : 37 + k] for k in range(4)]
    same = [reach[0] == reach[1], reach[2] == reach[3]]
    own = {}
    for k in range(4):
        for at in range(k * 9, k * 9 + 9):
            own[at] = spread[at : at + 1]
            if k % 2 == 0:
                own[at] = own[at] + jnp.where(same[k // 2], spread[at + 9 : at + 10], 0.0)
    tile = 16
    for c in range(3):
        lanes = slice(c * 128, (c + 1) * 128)
        wide = {at: jnp.broadcast_to(own[at][:, lanes], (tile, 128)) for at in own}
        goal = [jnp.broadcast_to(reach[k][:, lanes], (tile, 128)) for k in range(4)]
        for first_row in range(0, WIN, tile):
            slots = ((2, 3), (0, 1, 2, 3), (0, 1, 2, 3), (0, 1))[first_row // HALO]
            row = lax.broadcasted_iota(jnp.int32, (tile, 128), 0).astype(F32) + float(first_row)
            masks = {k: row == goal[k] for k in slots}
            for a in range(3):
                for q in range(3):
                    value = jnp.zeros((tile, 128), F32)
                    for k in reversed(slots):
                        value = jnp.where(masks[k], wide[(k * 3 + a) * 3 + q], value)
                    start = q * WIN + first_row
                    out_ref[0, a, start : start + tile, lanes] = value.astype(BF16)


def build_operator(place, couplings, neighbours, total_atoms):
    blocks = neighbours.shape[1] // BLOCK
    return pl.pallas_call(
        functools.partial(operator_kernel, total_atoms),
        grid=(blocks,),
        in_specs=[
            pl.BlockSpec(memory_space=pltpu.SMEM),
            pl.BlockSpec((4, 3, 3, 3, BLOCK), lambda i: (0, 0, 0, 0, i)),
            pl.BlockSpec((4, BLOCK), lambda i: (0, i)),
        ],
        out_specs=pl.BlockSpec((1, 3, 3 * WIN, ROWS), lambda i: (i, 0, 0, 0)),
        out_shape=jax.ShapeDtypeStruct((blocks, 3, 3 * WIN, ROWS), BF16),
        scratch_shapes=[pltpu.VMEM((40, BLOCK), F32)],
        compiler_params=pltpu.CompilerParams(vmem_limit_bytes=24 * 2**20),
        cost_estimate=pl.CostEstimate(flops=4 * 10**9, bytes_accessed=20 * 10**6, transcendentals=0),
    )(place, couplings, neighbours)


def copy_kernel(moves, *refs):
    for src, s0, dst, d0, n in moves:
        refs[dst][d0 : d0 + n, :] = refs[src][s0 : s0 + n, :]


def copied_rows(inputs, lengths, moves):
    width = inputs[0].shape[1]
    moves = [(i, s, len(inputs) + o, d, n) for i, s, o, d, n in moves]
    return pl.pallas_call(
        functools.partial(copy_kernel, moves),
        out_shape=[jax.ShapeDtypeStruct((n, width), inputs[0].dtype) for n in lengths],
    )(*inputs)


def star_step(planes_ref, start, operator_ref, partners, total_ref):
    window = [planes_ref[pl.ds(start + q, WIN, stride=3), :].astype(BF16) for q in range(3)]
    window = jnp.concatenate(window, axis=0).T
    applied = [jnp.dot(window, operator_ref[0, a], preferred_element_type=F32).astype(BF16) for a in range(3)]
    applied = jnp.concatenate(applied, axis=0)
    total_ref[...] += jnp.dot(applied, jnp.concatenate(partners, axis=1), preferred_element_type=F32)


def first_kernel(t_ref, far_ref, below_ref, above_ref, p0, p1, p2, p3, p4, out_ref, planes):
    g = pl.program_id(0)
    tail, edge = TAIL * ROWS, 3 * HALO

    @pl.when(g == 0)
    def _():
        out_ref[...] = jnp.zeros_like(out_ref)
        planes[0:tail, :] = far_ref[0:tail, :].astype(F32)
        planes[tail : tail + edge, :] = above_ref[...].astype(F32)
        planes[tail + edge : tail + 2 * edge, :] = below_ref[...].astype(F32)
        planes[tail + 2 * edge :, :] = far_ref[tail:, :].astype(F32)

    start = jnp.where(g < TAIL - 1, (g + 1) * ROWS - edge, tail + edge)
    star_step(planes, start, t_ref, [r[...] for r in (p0, p1, p2, p3, p4)], out_ref)


def second_kernel(
    place_ref, t_ref, before_ref, far_a, far_b, own, a0, a1, a2, a3, b0, b1, b2, b3, o0, o1, o2, o3, planes, total
):
    g = pl.program_id(0)
    steps = pl.num_programs(0)
    tail, head = TAIL * ROWS, HEAD * ROWS
    rows_b = far_b.shape[0]

    @pl.when(g == 0)
    def _():
        planes[0:head, :] = far_a[tail:, :].astype(F32)
        planes[head : head + rows_b, :] = far_b[...].astype(F32)
        planes[head + rows_b :, :] = far_a[0:tail, :].astype(F32)
        total[...] = before_ref[...]

    start = (g + 1) * ROWS - 3 * HALO
    in_first = jnp.logical_or(g == 0, g == steps - 1)

    @pl.when(in_first)
    def _():
        star_step(planes, start, t_ref, [a0[...], a1[...], own[...], a2[...], a3[...]], total)

    @pl.when(jnp.logical_not(in_first))
    def _():
        star_step(planes, start, t_ref, [b0[...], b1[...], own[...], b2[...], b3[...]], total)

    @pl.when(g == steps - 1)
    def _():
        for k, out in enumerate((o0, o1, o2, o3)):
            share = jnp.bitwise_xor(place_ref[0], k)
            for a in range(3):
                rows = pl.ds(pl.multiple_of(a * 128 + share * 32, 32), 32)
                out[a * 32 : (a + 1) * 32, :] = total[rows, :].astype(BF16)


def star_products(place, operator, own, below, above, firsts, seconds):
    blocks = operator.shape[0]
    width = own.shape[1]
    op_block = (1, 3, 3 * WIN, ROWS)
    shape = (3 * width, SLOTS * width)
    whole = lambda x: pl.BlockSpec(x.shape, lambda g: (0,) * x.ndim)
    cost = lambda n: pl.CostEstimate(flops=n * 10**9, bytes_accessed=n * 3 * 10**6, transcendentals=0)
    at = lambda g: lax.rem(g + blocks - TAIL + 1, blocks)
    in_a = pl.BlockSpec((ROWS, width), lambda g: (g + 1, 0))
    before = pl.pallas_call(
        first_kernel,
        grid=(TAIL,),
        in_specs=[pl.BlockSpec(op_block, lambda g: (at(g), 0, 0, 0)), whole(firsts[0]), whole(below), whole(above)]
        + [in_a, in_a, pl.BlockSpec((ROWS, width), lambda g: (at(g), 0)), in_a, in_a],
        out_specs=pl.BlockSpec(shape, lambda g: (0, 0)),
        out_shape=jax.ShapeDtypeStruct(shape, F32),
        scratch_shapes=[pltpu.VMEM((firsts[0].shape[0] + 6 * HALO, width), F32)],
        compiler_params=pltpu.CompilerParams(vmem_limit_bytes=24 * 2**20),
        cost_estimate=cost(TAIL),
    )(operator, firsts[0], below, above, firsts[0], firsts[1], own, firsts[2], firsts[3])
    steps = blocks - TAIL
    in_a = pl.BlockSpec((ROWS, width), lambda g: (jnp.where(g == steps - 1, 0, TAIL + HEAD - 1), 0))
    in_b = pl.BlockSpec((ROWS, width), lambda g: (jnp.clip(g - 1, 0, steps - 3), 0))
    out_shape = (shape[0] // 4, shape[1])
    return pl.pallas_call(
        second_kernel,
        grid=(steps,),
        in_specs=[
            pl.BlockSpec(memory_space=pltpu.SMEM),
            pl.BlockSpec(op_block, lambda g: (g + 1, 0, 0, 0)),
            pl.BlockSpec(shape, lambda g: (0, 0)),
            whole(firsts[0]),
            whole(seconds[0]),
            pl.BlockSpec((ROWS, width), lambda g: (g + 1, 0)),
        ]
        + [in_a] * 4
        + [in_b] * 4,
        out_specs=[pl.BlockSpec(out_shape, lambda g: (0, 0))] * 4,
        out_shape=[jax.ShapeDtypeStruct(out_shape, BF16)] * 4,
        scratch_shapes=[pltpu.VMEM((blocks * ROWS, width), F32), pltpu.VMEM(shape, F32)],
        compiler_params=pltpu.CompilerParams(vmem_limit_bytes=32 * 2**20),
        cost_estimate=cost(steps),
    )(place, operator, before, firsts[0], seconds[0], own, *firsts, *seconds)


RETURNS = (1, -1, 2, -2)


def weigh_kernel(half_width, place_ref, s0, s1, s2, s3, freq_ref, o0, o1, o2, o3, stay_ref, rows_ref):
    atom, mode = place_ref[0], place_ref[1]
    modes = freq_ref.shape[0]
    summed = s0[...].astype(F32) + s1[...].astype(F32) + s2[...].astype(F32) + s3[...].astype(F32)
    squares = summed[0:32] * summed[0:32] + summed[32:64] * summed[32:64] + summed[64:96] * summed[64:96]
    row = lax.broadcasted_iota(jnp.int32, (32, 128), 0) + 32 * atom
    lane = lax.broadcasted_iota(jnp.int32, (32, 128), 1)
    wrapped = lambda b: jnp.where(b >= modes, b - modes, jnp.where(b < 0, b + modes, b))
    top = wrapped(mode + 2)
    top_freq = freq_ref[pl.ds(top, 1), :]
    centre = jnp.sum(jnp.where(row == lane, top_freq, 0.0), axis=1, keepdims=True)
    own = jnp.zeros((32, 128), F32)
    for slot in range(SLOTS):
        block = wrapped(mode + 2 - slot)
        offset = centre - freq_ref[pl.ds(block, 1), :]
        lorentz = (half_width / math.pi) / (offset * offset + half_width * half_width)
        term = jnp.where(block <= top, squares[:, slot * 128 : (slot + 1) * 128] * lorentz, 0.0)
        own += term
        if slot == 2:
            stay_ref[...] = jnp.sum(term, axis=0, keepdims=True)
        elif slot > 0:
            at = RETURNS.index(2 - slot)
            rows_ref[at : at + 1, :] = jnp.sum(term, axis=0, keepdims=True)
    own = jnp.sum(own, axis=1, keepdims=True)
    at = RETURNS.index(2)
    rows_ref[at : at + 1, :] = jnp.sum(jnp.where(row == lane, own, 0.0), axis=0, keepdims=True)
    for k, out in enumerate((o0, o1, o2, o3)):
        out[...] = rows_ref[pl.ds(jnp.bitwise_xor(atom, k), 1), :]


def swapped(x, k):
    return lax.ppermute(x, "atom", [(i, i ^ k) for i in range(4)])


def local(vectors, couplings, neighbours, frequency):
    rows_dev, width = vectors.shape
    atoms_dev = rows_dev // 3
    atom_groups = lax.axis_size("atom")
    modes = lax.axis_size("mode")
    half_width = WIDTH_MODES / (width * modes)
    place = jnp.stack([lax.axis_index("atom"), lax.axis_index("mode")]).astype(jnp.int32)
    edge = 3 * HALO
    head, tail = HEAD * ROWS, TAIL * ROWS
    rest = rows_dev - head - tail
    own_a, own_b = copied_rows(
        [vectors],
        [head + tail, rest],
        [(0, rows_dev - tail, 0, 0, tail), (0, 0, 0, tail, head), (0, head, 1, 0, rest)],
    )
    up1a = shifted(own_a, "mode", -1)
    dn1a = shifted(own_a, "mode", 1)
    up1b = shifted(own_b, "mode", -1)
    dn1b = shifted(own_b, "mode", 1)
    operator = build_operator(place, couplings, neighbours, atoms_dev * atom_groups)
    up1a, dn1a, operator = lax.optimization_barrier((up1a, dn1a, operator))
    up2a = shifted(up1a, "mode", -1)
    dn2a = shifted(dn1a, "mode", 1)
    up2b = shifted(up1b, "mode", -1)
    dn2b = shifted(dn1b, "mode", 1)
    below = shifted(up2a[tail - edge : tail], "atom", 1)
    above = shifted(up2a[tail : tail + edge], "atom", -1)

    shares = star_products(
        place, operator, vectors, below, above, [up2a, up1a, dn1a, dn2a], [up2b, up1b, dn1b, dn2b]
    )
    shares = [shares[0]] + [swapped(shares[k], k) for k in range(1, 4)]

    vmem = pl.BlockSpec(memory_space=pltpu.VMEM)
    row = jax.ShapeDtypeStruct((1, width), F32)
    *terms, stay = pl.pallas_call(
        functools.partial(weigh_kernel, half_width),
        in_specs=[pl.BlockSpec(memory_space=pltpu.SMEM)] + [vmem] * 5,
        out_specs=[vmem] * 5,
        out_shape=[row] * 5,
        scratch_shapes=[pltpu.VMEM((4, width), F32)],
    )(place, *shares, frequency.reshape(modes, width))
    carried = terms[0]
    for k in range(1, 4):
        carried = carried + swapped(terms[k], k)
    route = [(b * 4 + s, (b + RETURNS[s]) % modes * 4 + s) for b in range(modes) for s in range(4)]
    result = stay + lax.ppermute(carried, ("mode", "atom"), route)
    far = [swapped(result, k) for k in range(1, 4)]
    total = (result + far[0]) + (far[1] + far[2])
    own_freq = lax.dynamic_slice_in_dim(frequency, place[1] * width, width)
    return math.pi / (3.0 * own_freq * own_freq) * total.reshape(width)


def solution(mesh):
    return jax.shard_map(
        local,
        mesh=mesh,
        in_specs=(P("atom", "mode"), P(None, None, None, None, "atom"), P(None, "atom"), P()),
        out_specs=P("mode"),
        check_vma=False,
    )
```

```python
import functools
import math

import jax
import jax.numpy as jnp
from jax import lax
from jax.experimental import pallas as pl
from jax.experimental.pallas import tpu as pltpu
from jax.sharding import PartitionSpec as P

HALO = 64
PARTNERS = 4
WIDTH_MODES = 320
BLOCK = 128
WIN = BLOCK + 2 * HALO
ROWS = 3 * BLOCK
HEAD, TAIL = 2, 3
SLOTS = 5
TABLE = 40
F32, BF16 = jnp.float32, jnp.bfloat16


def shifted(x, axis, distance):
    count = lax.axis_size(axis)
    return lax.ppermute(x, axis, [(i, (i + distance) % count) for i in range(count)])


def table_kernel(total_atoms, place_ref, couplings_ref, neighbours_ref, out_ref, rows_ref):
    blocks = neighbours_ref.shape[1] // BLOCK
    lane = lax.broadcasted_iota(jnp.int32, (BLOCK, ROWS), 1)
    atom = lax.broadcasted_iota(jnp.int32, (BLOCK, ROWS), 0)
    spread = jnp.zeros((blocks * TABLE, ROWS), F32)
    for p in range(3):
        for i in range(blocks):
            lanes = slice(i * BLOCK, (i + 1) * BLOCK)
            for k in range(4):
                for a in range(3):
                    at = i * TABLE + (k * 3 + a) * 3
                    rows_ref[at : at + 3, :] = couplings_ref[k, a, p, :, lanes]
            target = neighbours_ref[:, lanes] - ((place_ref[0] * blocks + i) * BLOCK - HALO)
            target = jnp.where(target < 0, target + total_atoms, target)
            target = jnp.where(target >= total_atoms, target - total_atoms, target)
            rows_ref[i * TABLE + 36 : (i + 1) * TABLE, :] = target.astype(F32)
        place = jnp.where(lane == 3 * atom + p, 1.0, 0.0).astype(BF16)
        spread += jnp.dot(rows_ref[...].astype(BF16), place, preferred_element_type=F32)
    for i in range(blocks):
        rows = spread[i * TABLE : (i + 1) * TABLE]
        out_ref[i] = rows
        for k in (0, 2):
            same = rows[36 + k : 37 + k] == rows[37 + k : 38 + k]
            twin = jnp.where(same, rows[(k + 1) * 9 : (k + 2) * 9], 0.0)
            out_ref[i, k * 9 : (k + 1) * 9, :] = rows[k * 9 : (k + 1) * 9] + twin


def operator_table(place, couplings, neighbours, total_atoms):
    blocks = neighbours.shape[1] // BLOCK
    vmem = pl.BlockSpec(memory_space=pltpu.VMEM)
    return pl.pallas_call(
        functools.partial(table_kernel, total_atoms),
        in_specs=[pl.BlockSpec(memory_space=pltpu.SMEM), vmem, vmem],
        out_shape=jax.ShapeDtypeStruct((blocks, TABLE, ROWS), F32),
        scratch_shapes=[pltpu.VMEM((blocks * TABLE, BLOCK), F32)],
        compiler_params=pltpu.CompilerParams(vmem_limit_bytes=16 * 2**20),
        cost_estimate=pl.CostEstimate(flops=2 * 10**9, bytes_accessed=3 * 10**6, transcendentals=0),
    )(place, couplings, neighbours)


TILE = 16


def tile_slots(first_row, first_lane):
    low, high = first_lane // 3 + HALO, (first_lane + 127) // 3 + HALO
    meets = lambda lo, hi: first_row <= hi and lo < first_row + TILE
    up = (0, 1) if meets(low + 2, high + HALO) else ()
    return up + ((2, 3) if meets(low - HALO, high - 2) else ())


def fill_operator(table_ref, operator_ref):
    for first_lane in range(0, ROWS, 128):
        lanes = slice(first_lane, first_lane + 128)
        wide = [jnp.broadcast_to(table_ref[0, at : at + 1, lanes], (TILE, 128)).astype(BF16) for at in range(TABLE)]
        for first_row in range(0, WIN, TILE):
            slots = tile_slots(first_row, first_lane)
            if not slots:
                continue
            row = (lax.broadcasted_iota(jnp.int32, (TILE, 128), 0).astype(F32) + float(first_row)).astype(BF16)
            masks = {k: row == wide[36 + k] for k in slots}
            for a in range(3):
                for q in range(3):
                    value = jnp.zeros((TILE, 128), BF16)
                    for k in reversed(slots):
                        value = jnp.where(masks[k], wide[(k * 3 + a) * 3 + q], value)
                    start = q * WIN + first_row
                    operator_ref[start : start + TILE, a * ROWS + first_lane : a * ROWS + first_lane + 128] = value


def copy_kernel(moves, *refs):
    for src, s0, dst, d0, n in moves:
        refs[dst][d0 : d0 + n, :] = refs[src][s0 : s0 + n, :]


def copied_rows(inputs, lengths, moves):
    width = inputs[0].shape[1]
    moves = [(i, s, len(inputs) + o, d, n) for i, s, o, d, n in moves]
    return pl.pallas_call(
        functools.partial(copy_kernel, moves),
        out_shape=[jax.ShapeDtypeStruct((n, width), inputs[0].dtype) for n in lengths],
        compiler_params=pltpu.CompilerParams(vmem_limit_bytes=8 * 2**20),
    )(*inputs)


def star_step(planes_ref, start, table_ref, operator_ref, partners, total_ref):
    fill_operator(table_ref, operator_ref)
    window = [planes_ref[pl.ds(start + q, WIN, stride=3), :].astype(BF16) for q in range(3)]
    window = jnp.concatenate(window, axis=0).T
    applied = jnp.dot(window, operator_ref[...], preferred_element_type=F32).astype(BF16)
    applied = jnp.concatenate([applied[:, a * ROWS : (a + 1) * ROWS] for a in range(3)], axis=0)
    total_ref[...] += jnp.dot(applied, jnp.concatenate(partners, axis=1), preferred_element_type=F32)


def first_kernel(t_ref, far_ref, below_ref, above_ref, p0, p1, p2, p3, p4, out_ref, planes, dense):
    g = pl.program_id(0)
    tail, edge = TAIL * ROWS, 3 * HALO

    @pl.when(g == 0)
    def _():
        out_ref[...] = jnp.zeros_like(out_ref)
        dense[...] = jnp.zeros_like(dense)
        planes[0:tail, :] = far_ref[0:tail, :].astype(F32)
        planes[tail : tail + edge, :] = above_ref[...].astype(F32)
        planes[tail + edge : tail + 2 * edge, :] = below_ref[...].astype(F32)
        planes[tail + 2 * edge :, :] = far_ref[tail:, :].astype(F32)

    start = jnp.where(g < TAIL - 1, (g + 1) * ROWS - edge, tail + edge)
    star_step(planes, start, t_ref, dense, [r[...] for r in (p0, p1, p2, p3, p4)], out_ref)


def second_kernel(
    place_ref, t_ref, before_ref, far_a, far_b, own, a0, a1, a2, a3, b0, b1, b2, b3, o0, o1, o2, o3, planes, total, dense
):
    g = pl.program_id(0)
    steps = pl.num_programs(0)
    tail, head = TAIL * ROWS, HEAD * ROWS
    rows_b = far_b.shape[0]

    @pl.when(g == 0)
    def _():
        planes[0:head, :] = far_a[tail:, :].astype(F32)
        planes[head : head + rows_b, :] = far_b[...].astype(F32)
        planes[head + rows_b :, :] = far_a[0:tail, :].astype(F32)
        total[...] = before_ref[...]
        dense[...] = jnp.zeros_like(dense)

    start = (g + 1) * ROWS - 3 * HALO
    in_first = jnp.logical_or(g == 0, g == steps - 1)

    @pl.when(in_first)
    def _():
        star_step(planes, start, t_ref, dense, [a0[...], a1[...], own[...], a2[...], a3[...]], total)

    @pl.when(jnp.logical_not(in_first))
    def _():
        star_step(planes, start, t_ref, dense, [b0[...], b1[...], own[...], b2[...], b3[...]], total)

    @pl.when(g == steps - 1)
    def _():
        for k, out in enumerate((o0, o1, o2, o3)):
            share = jnp.bitwise_xor(place_ref[0], k)
            for a in range(3):
                rows = pl.ds(pl.multiple_of(a * 128 + share * 32, 32), 32)
                out[a * 32 : (a + 1) * 32, :] = total[rows, :].astype(BF16)


def star_products(place, operator, own, below, above, firsts, seconds):
    blocks = operator.shape[0]
    width = own.shape[1]
    op_block = (1, TABLE, ROWS)
    dense = pltpu.VMEM((3 * WIN, 3 * ROWS), BF16)
    shape = (3 * width, SLOTS * width)
    whole = lambda x: pl.BlockSpec(x.shape, lambda g: (0,) * x.ndim)
    cost = lambda n: pl.CostEstimate(flops=n * 10**9, bytes_accessed=n * 3 * 10**6, transcendentals=0)
    at = lambda g: lax.rem(g + blocks - TAIL + 1, blocks)
    in_a = pl.BlockSpec((ROWS, width), lambda g: (g + 1, 0))
    before = pl.pallas_call(
        first_kernel,
        grid=(TAIL,),
        in_specs=[pl.BlockSpec(op_block, lambda g: (at(g), 0, 0)), whole(firsts[0]), whole(below), whole(above)]
        + [in_a, in_a, pl.BlockSpec((ROWS, width), lambda g: (at(g), 0)), in_a, in_a],
        out_specs=pl.BlockSpec(shape, lambda g: (0, 0)),
        out_shape=jax.ShapeDtypeStruct(shape, F32),
        scratch_shapes=[pltpu.VMEM((firsts[0].shape[0] + 6 * HALO, width), F32), dense],
        compiler_params=pltpu.CompilerParams(vmem_limit_bytes=24 * 2**20),
        cost_estimate=cost(TAIL),
    )(operator, firsts[0], below, above, firsts[0], firsts[1], own, firsts[2], firsts[3])
    steps = blocks - TAIL
    in_a = pl.BlockSpec((ROWS, width), lambda g: (jnp.where(g == steps - 1, 0, TAIL + HEAD - 1), 0))
    in_b = pl.BlockSpec((ROWS, width), lambda g: (jnp.clip(g - 1, 0, steps - 3), 0))
    out_shape = (shape[0] // 4, shape[1])
    return pl.pallas_call(
        second_kernel,
        grid=(steps,),
        in_specs=[
            pl.BlockSpec(memory_space=pltpu.SMEM),
            pl.BlockSpec(op_block, lambda g: (g + 1, 0, 0)),
            pl.BlockSpec(shape, lambda g: (0, 0)),
            whole(firsts[0]),
            whole(seconds[0]),
            pl.BlockSpec((ROWS, width), lambda g: (g + 1, 0)),
        ]
        + [in_a] * 4
        + [in_b] * 4,
        out_specs=[pl.BlockSpec(out_shape, lambda g: (0, 0))] * 4,
        out_shape=[jax.ShapeDtypeStruct(out_shape, BF16)] * 4,
        scratch_shapes=[pltpu.VMEM((blocks * ROWS, width), F32), pltpu.VMEM(shape, F32), dense],
        compiler_params=pltpu.CompilerParams(vmem_limit_bytes=32 * 2**20),
        cost_estimate=cost(steps),
    )(place, operator, before, firsts[0], seconds[0], own, *firsts, *seconds)


RETURNS = (1, -1, 2, -2)


def weigh_kernel(half_width, place_ref, s0, s1, s2, s3, freq_ref, o0, o1, o2, o3, rows_ref):
    atom, mode = place_ref[0], place_ref[1]
    modes = freq_ref.shape[0]
    summed = s0[...].astype(F32) + s1[...].astype(F32) + s2[...].astype(F32) + s3[...].astype(F32)
    squares = summed[0:32] * summed[0:32] + summed[32:64] * summed[32:64] + summed[64:96] * summed[64:96]
    row = lax.broadcasted_iota(jnp.int32, (32, 128), 0) + 32 * atom
    lane = lax.broadcasted_iota(jnp.int32, (32, 128), 1)
    wrapped = lambda b: jnp.where(b >= modes, b - modes, jnp.where(b < 0, b + modes, b))
    top = wrapped(mode + 2)
    top_freq = freq_ref[pl.ds(top, 1), :]
    centre = jnp.sum(jnp.where(row == lane, top_freq, 0.0), axis=1, keepdims=True)
    own = jnp.zeros((32, 128), F32)
    for slot in range(SLOTS):
        block = wrapped(mode + 2 - slot)
        offset = centre - freq_ref[pl.ds(block, 1), :]
        lorentz = (half_width / math.pi) / (offset * offset + half_width * half_width)
        term = jnp.where(block <= top, squares[:, slot * 128 : (slot + 1) * 128] * lorentz, 0.0)
        own += term
        if slot == 2:
            rows_ref[4:5, :] = jnp.sum(term, axis=0, keepdims=True)
        elif slot > 0:
            at = RETURNS.index(2 - slot)
            rows_ref[at : at + 1, :] = jnp.sum(term, axis=0, keepdims=True)
    own = jnp.sum(own, axis=1, keepdims=True)
    at = RETURNS.index(2)
    rows_ref[at : at + 1, :] = jnp.sum(jnp.where(row == lane, own, 0.0), axis=0, keepdims=True)
    for k, out in enumerate((o0, o1, o2, o3)):
        out[0:1, :] = rows_ref[pl.ds(jnp.bitwise_xor(atom, k), 1), :]
        out[1:2, :] = rows_ref[4:5, :]


def swapped(x, k):
    return lax.ppermute(x, "atom", [(i, i ^ k) for i in range(4)])


def local(vectors, couplings, neighbours, frequency):
    rows_dev, width = vectors.shape
    atoms_dev = rows_dev // 3
    atom_groups = lax.axis_size("atom")
    modes = lax.axis_size("mode")
    half_width = WIDTH_MODES / (width * modes)
    place = jnp.stack([lax.axis_index("atom"), lax.axis_index("mode")]).astype(jnp.int32)
    edge = 3 * HALO
    head, tail = HEAD * ROWS, TAIL * ROWS
    rest = rows_dev - head - tail
    own_a, own_b = copied_rows(
        [vectors],
        [head + tail, rest],
        [(0, rows_dev - tail, 0, 0, tail), (0, 0, 0, tail, head), (0, head, 1, 0, rest)],
    )
    up1a = shifted(own_a, "mode", -1)
    dn1a = shifted(own_a, "mode", 1)
    up1b = shifted(own_b, "mode", -1)
    dn1b = shifted(own_b, "mode", 1)
    operator = operator_table(place, couplings, neighbours, atoms_dev * atom_groups)
    up1a, dn1a, operator = lax.optimization_barrier((up1a, dn1a, operator))
    up2a = shifted(up1a, "mode", -1)
    dn2a = shifted(dn1a, "mode", 1)
    up2b = shifted(up1b, "mode", -1)
    dn2b = shifted(dn1b, "mode", 1)
    below = shifted(up2a[tail - edge : tail], "atom", 1)
    above = shifted(up2a[tail : tail + edge], "atom", -1)

    shares = star_products(
        place, operator, vectors, below, above, [up2a, up1a, dn1a, dn2a], [up2b, up1b, dn1b, dn2b]
    )
    shares = [shares[0]] + [swapped(shares[k], k) for k in range(1, 4)]

    own_freq = lax.dynamic_slice_in_dim(frequency, place[1] * width, width)
    factor, seconds_done = lax.optimization_barrier((math.pi / (3.0 * own_freq * own_freq), shares[0]))
    shares[0] = seconds_done
    whole = lambda shape: pl.BlockSpec(shape, lambda g: (0, 0))
    freq_rows = frequency.reshape(modes, width)
    pair = jax.ShapeDtypeStruct((2, width), F32)
    terms = pl.pallas_call(
        functools.partial(weigh_kernel, half_width),
        grid=(1,),
        in_specs=[pl.BlockSpec(memory_space=pltpu.SMEM)] + [whole(x.shape) for x in (*shares, freq_rows)],
        out_specs=[whole(pair.shape)] * 4,
        out_shape=[pair] * 4,
        scratch_shapes=[pltpu.VMEM((5, width), F32)],
        compiler_params=pltpu.CompilerParams(vmem_limit_bytes=4 * 2**20),
    )(place, *shares, freq_rows)
    arrived = [terms[0]] + [swapped(terms[k], k) for k in range(1, 4)]
    carried = (arrived[0] + arrived[1]) + (arrived[2] + arrived[3])
    route = [(b * 4 + s, (b + RETURNS[s]) % modes * 4 + s) for b in range(modes) for s in range(4)]
    result = lax.ppermute(carried[0], ("mode", "atom"), route)
    far = [swapped(result, k) for k in range(1, 4)]
    return factor * (carried[1] + ((result + far[0]) + (far[1] + far[2])))


def solution(mesh):
    return jax.shard_map(
        local,
        mesh=mesh,
        in_specs=(P("atom", "mode"), P(None, None, None, None, "atom"), P(None, "atom"), P()),
        out_specs=P("mode"),
        check_vma=False,
    )
```

```python
import functools
import math

import jax
import jax.numpy as jnp
from jax import lax
from jax.experimental import pallas as pl
from jax.experimental.pallas import tpu as pltpu
from jax.sharding import PartitionSpec as P

HALO = 64
PARTNERS = 4
WIDTH_MODES = 320
BLOCK = 128
WIN = BLOCK + 2 * HALO
ROWS = 3 * BLOCK
HEAD, TAIL = 2, 3
SLOTS = 5
TABLE = 40
F32, BF16 = jnp.float32, jnp.bfloat16


def shifted(x, axis, distance):
    count = lax.axis_size(axis)
    return lax.ppermute(x, axis, [(i, (i + distance) % count) for i in range(count)])


def table_kernel(total_atoms, place_ref, couplings_ref, neighbours_ref, out_ref, rows_ref):
    blocks = neighbours_ref.shape[1] // BLOCK
    lane = lax.broadcasted_iota(jnp.int32, (BLOCK, ROWS), 1)
    atom = lax.broadcasted_iota(jnp.int32, (BLOCK, ROWS), 0)
    spread = jnp.zeros((blocks * TABLE, ROWS), F32)
    for p in range(3):
        for i in range(blocks):
            lanes = slice(i * BLOCK, (i + 1) * BLOCK)
            for k in range(4):
                for a in range(3):
                    at = i * TABLE + (k * 3 + a) * 3
                    rows_ref[at : at + 3, :] = couplings_ref[k, a, p, :, lanes]
            target = neighbours_ref[:, lanes] - ((place_ref[0] * blocks + i) * BLOCK - HALO)
            target = jnp.where(target < 0, target + total_atoms, target)
            target = jnp.where(target >= total_atoms, target - total_atoms, target)
            rows_ref[i * TABLE + 36 : (i + 1) * TABLE, :] = target.astype(F32)
        place = jnp.where(lane == 3 * atom + p, 1.0, 0.0).astype(BF16)
        spread += jnp.dot(rows_ref[...].astype(BF16), place, preferred_element_type=F32)
    for i in range(blocks):
        rows = spread[i * TABLE : (i + 1) * TABLE]
        out_ref[i] = rows
        for k in (0, 2):
            same = rows[36 + k : 37 + k] == rows[37 + k : 38 + k]
            twin = jnp.where(same, rows[(k + 1) * 9 : (k + 2) * 9], 0.0)
            out_ref[i, k * 9 : (k + 1) * 9, :] = rows[k * 9 : (k + 1) * 9] + twin


def operator_table(place, couplings, neighbours, total_atoms):
    blocks = neighbours.shape[1] // BLOCK
    vmem = pl.BlockSpec(memory_space=pltpu.VMEM)
    return pl.pallas_call(
        functools.partial(table_kernel, total_atoms),
        in_specs=[pl.BlockSpec(memory_space=pltpu.SMEM), vmem, vmem],
        out_shape=jax.ShapeDtypeStruct((blocks, TABLE, ROWS), F32),
        scratch_shapes=[pltpu.VMEM((blocks * TABLE, BLOCK), F32)],
        compiler_params=pltpu.CompilerParams(vmem_limit_bytes=16 * 2**20),
        cost_estimate=pl.CostEstimate(flops=2 * 10**9, bytes_accessed=3 * 10**6, transcendentals=0),
    )(place, couplings, neighbours)


TILE = 16


def tile_slots(first_row, first_lane):
    low, high = first_lane // 3 + HALO, (first_lane + 127) // 3 + HALO
    meets = lambda lo, hi: first_row <= hi and lo < first_row + TILE
    up = (0, 1) if meets(low + 2, high + HALO) else ()
    return up + ((2, 3) if meets(low - HALO, high - 2) else ())


def fill_kernel(table_ref, out_ref):
    for block in range(table_ref.shape[0]):
        for first_lane in range(0, ROWS, 128):
            lanes = slice(first_lane, first_lane + 128)
            wide = [
                jnp.broadcast_to(table_ref[block, at : at + 1, lanes], (TILE, 128)).astype(BF16) for at in range(TABLE)
            ]
            for first_row in range(0, WIN, TILE):
                slots = tile_slots(first_row, first_lane)
                row = (lax.broadcasted_iota(jnp.int32, (TILE, 128), 0).astype(F32) + float(first_row)).astype(BF16)
                masks = {k: row == wide[36 + k] for k in slots}
                for a in range(3):
                    for q in range(3):
                        value = jnp.zeros((TILE, 128), BF16)
                        for k in reversed(slots):
                            value = jnp.where(masks[k], wide[(k * 3 + a) * 3 + q], value)
                        start, lane = q * WIN + first_row, a * ROWS + first_lane
                        out_ref[block, start : start + TILE, lane : lane + 128] = value


def filled_operator(table):
    vmem = pl.BlockSpec(memory_space=pltpu.VMEM)
    return pl.pallas_call(
        fill_kernel,
        in_specs=[vmem],
        out_specs=vmem,
        out_shape=jax.ShapeDtypeStruct((table.shape[0], 3 * WIN, 3 * ROWS), BF16),
        compiler_params=pltpu.CompilerParams(vmem_limit_bytes=8 * 2**20),
        cost_estimate=pl.CostEstimate(flops=4 * 10**9, bytes_accessed=10**6, transcendentals=0),
    )(table)


def copy_kernel(moves, *refs):
    for src, s0, dst, d0, n in moves:
        refs[dst][d0 : d0 + n, :] = refs[src][s0 : s0 + n, :]


def copied_rows(inputs, lengths, moves):
    width = inputs[0].shape[1]
    moves = [(i, s, len(inputs) + o, d, n) for i, s, o, d, n in moves]
    return pl.pallas_call(
        functools.partial(copy_kernel, moves),
        out_shape=[jax.ShapeDtypeStruct((n, width), inputs[0].dtype) for n in lengths],
        compiler_params=pltpu.CompilerParams(vmem_limit_bytes=8 * 2**20),
    )(*inputs)


def star_step(planes_ref, start, operator_ref, partners, total_ref):
    window = [planes_ref[pl.ds(start + q, WIN, stride=3), :].astype(BF16) for q in range(3)]
    window = jnp.concatenate(window, axis=0).T
    applied = jnp.dot(window, operator_ref[...], preferred_element_type=F32).astype(BF16)
    applied = jnp.concatenate([applied[:, a * ROWS : (a + 1) * ROWS] for a in range(3)], axis=0)
    total_ref[...] += jnp.dot(applied, jnp.concatenate(partners, axis=1), preferred_element_type=F32)


def first_kernel(t_ref, far_ref, below_ref, above_ref, p1, own, p2, p3, out_ref, planes):
    tail, edge = TAIL * ROWS, 3 * HALO
    out_ref[...] = jnp.zeros_like(out_ref)
    planes[0:tail, :] = far_ref[0:tail, :].astype(F32)
    planes[tail : tail + edge, :] = above_ref[...].astype(F32)
    planes[tail + edge : tail + 2 * edge, :] = below_ref[...].astype(F32)
    planes[tail + 2 * edge :, :] = far_ref[tail:, :].astype(F32)
    blocks = own.shape[0] // ROWS
    for at in range(ROWS, tail + ROWS, ROWS):
        block = (blocks - TAIL + at // ROWS) % blocks
        near = [r[at : at + ROWS, :] for r in (far_ref, p1, p2, p3)]
        near.insert(2, own[block * ROWS : (block + 1) * ROWS, :])
        star_step(planes, at - edge if block else tail + edge, t_ref.at[block], near, out_ref)


def second_kernel(
    place_ref, t_ref, before_ref, far_a, far_b, own, a1, a2, a3, b1, b2, b3, o0, o1, o2, o3, planes, total
):
    tail, head = TAIL * ROWS, HEAD * ROWS
    rows_b = far_b.shape[0]
    planes[0:head, :] = far_a[tail:, :].astype(F32)
    planes[head : head + rows_b, :] = far_b[...].astype(F32)
    planes[head + rows_b :, :] = far_a[0:tail, :].astype(F32)
    total[...] = before_ref[...]
    blocks = own.shape[0] // ROWS
    for block in range(1, blocks - TAIL + 1):
        if block < HEAD or block >= blocks - TAIL:
            at = tail + block * ROWS if block < HEAD else (block - blocks + TAIL) * ROWS
            near = [r[at : at + ROWS, :] for r in (far_a, a1, a2, a3)]
        else:
            at = (block - HEAD) * ROWS
            near = [r[at : at + ROWS, :] for r in (far_b, b1, b2, b3)]
        near.insert(2, own[block * ROWS : (block + 1) * ROWS, :])
        star_step(planes, block * ROWS - 3 * HALO, t_ref.at[block], near, total)
    for k, out in enumerate((o0, o1, o2, o3)):
        share = jnp.bitwise_xor(place_ref[0], k)
        for a in range(3):
            rows = pl.ds(pl.multiple_of(a * 128 + share * 32, 32), 32)
            out[a * 32 : (a + 1) * 32, :] = total[rows, :].astype(BF16)


def star_products(place, operator, own, below, above, firsts, seconds):
    blocks = operator.shape[0]
    width = own.shape[1]
    shape = (3 * width, SLOTS * width)
    vmem = pl.BlockSpec(memory_space=pltpu.VMEM)
    cost = lambda n: pl.CostEstimate(flops=n * 10**9, bytes_accessed=n * 3 * 10**6, transcendentals=0)
    before = pl.pallas_call(
        first_kernel,
        in_specs=[vmem] * 8,
        out_specs=vmem,
        out_shape=jax.ShapeDtypeStruct(shape, F32),
        scratch_shapes=[pltpu.VMEM((firsts[0].shape[0] + 6 * HALO, width), F32)],
        compiler_params=pltpu.CompilerParams(vmem_limit_bytes=10 * 2**20),
        cost_estimate=cost(TAIL),
    )(operator, firsts[0], below, above, firsts[1], own, *firsts[2:])
    steps = blocks - TAIL
    out_shape = (shape[0] // 4, shape[1])
    return pl.pallas_call(
        second_kernel,
        in_specs=[pl.BlockSpec(memory_space=pltpu.SMEM)] + [vmem] * 11,
        out_specs=[vmem] * 4,
        out_shape=[jax.ShapeDtypeStruct(out_shape, BF16)] * 4,
        scratch_shapes=[pltpu.VMEM((blocks * ROWS, width), F32), pltpu.VMEM(shape, F32)],
        compiler_params=pltpu.CompilerParams(vmem_limit_bytes=12 * 2**20),
        cost_estimate=cost(steps),
    )(place, operator, before, firsts[0], seconds[0], own, *firsts[1:], *seconds[1:])


RETURNS = (1, -1, 2, -2)


def weigh_kernel(half_width, place_ref, s0, s1, s2, s3, freq_ref, o0, o1, o2, o3, rows_ref):
    atom, mode = place_ref[0], place_ref[1]
    modes = freq_ref.shape[0]
    summed = s0[...].astype(F32) + s1[...].astype(F32) + s2[...].astype(F32) + s3[...].astype(F32)
    squares = summed[0:32] * summed[0:32] + summed[32:64] * summed[32:64] + summed[64:96] * summed[64:96]
    row = lax.broadcasted_iota(jnp.int32, (32, 128), 0) + 32 * atom
    lane = lax.broadcasted_iota(jnp.int32, (32, 128), 1)
    wrapped = lambda b: jnp.where(b >= modes, b - modes, jnp.where(b < 0, b + modes, b))
    top = wrapped(mode + 2)
    top_freq = freq_ref[pl.ds(top, 1), :]
    centre = jnp.sum(jnp.where(row == lane, top_freq, 0.0), axis=1, keepdims=True)
    own = jnp.zeros((32, 128), F32)
    for slot in range(SLOTS):
        block = wrapped(mode + 2 - slot)
        offset = centre - freq_ref[pl.ds(block, 1), :]
        lorentz = (half_width / math.pi) / (offset * offset + half_width * half_width)
        term = jnp.where(block <= top, squares[:, slot * 128 : (slot + 1) * 128] * lorentz, 0.0)
        own += term
        if slot == 2:
            rows_ref[4:5, :] = jnp.sum(term, axis=0, keepdims=True)
        elif slot > 0:
            at = RETURNS.index(2 - slot)
            rows_ref[at : at + 1, :] = jnp.sum(term, axis=0, keepdims=True)
    own = jnp.sum(own, axis=1, keepdims=True)
    at = RETURNS.index(2)
    rows_ref[at : at + 1, :] = jnp.sum(jnp.where(row == lane, own, 0.0), axis=0, keepdims=True)
    for k, out in enumerate((o0, o1, o2, o3)):
        out[0:1, :] = rows_ref[pl.ds(jnp.bitwise_xor(atom, k), 1), :]
        out[1:2, :] = rows_ref[4:5, :]


def swapped(x, k):
    return lax.ppermute(x, "atom", [(i, i ^ k) for i in range(4)])


def local(vectors, couplings, neighbours, frequency):
    rows_dev, width = vectors.shape
    atoms_dev = rows_dev // 3
    atom_groups = lax.axis_size("atom")
    modes = lax.axis_size("mode")
    half_width = WIDTH_MODES / (width * modes)
    place = jnp.stack([lax.axis_index("atom"), lax.axis_index("mode")]).astype(jnp.int32)
    edge = 3 * HALO
    head, tail = HEAD * ROWS, TAIL * ROWS
    rest = rows_dev - head - tail
    own_a, own_b = copied_rows(
        [vectors],
        [head + tail, rest],
        [(0, rows_dev - tail, 0, 0, tail), (0, 0, 0, tail, head), (0, head, 1, 0, rest)],
    )
    up1a = shifted(own_a, "mode", -1)
    dn1a = shifted(own_a, "mode", 1)
    up1b = shifted(own_b, "mode", -1)
    dn1b = shifted(own_b, "mode", 1)
    operator = operator_table(place, couplings, neighbours, atoms_dev * atom_groups)
    up1a, dn1a, operator = lax.optimization_barrier((up1a, dn1a, operator))
    up2a = shifted(up1a, "mode", -1)
    dn2a = shifted(dn1a, "mode", 1)
    up2b = shifted(up1b, "mode", -1)
    dn2b = shifted(dn1b, "mode", 1)
    below = shifted(up2a[tail - edge : tail], "atom", 1)
    above = shifted(up2a[tail : tail + edge], "atom", -1)

    operator, up2a = lax.optimization_barrier((operator, up2a))
    operator = filled_operator(operator)
    shares = star_products(
        place, operator, vectors, below, above, [up2a, up1a, dn1a, dn2a], [up2b, up1b, dn1b, dn2b]
    )
    shares = [shares[0]] + [swapped(shares[k], k) for k in range(1, 4)]

    own_freq = lax.dynamic_slice_in_dim(frequency, place[1] * width, width)
    factor, seconds_done = lax.optimization_barrier((math.pi / (3.0 * own_freq * own_freq), shares[0]))
    shares[0] = seconds_done
    whole = lambda shape: pl.BlockSpec(shape, lambda g: (0, 0))
    freq_rows = frequency.reshape(modes, width)
    pair = jax.ShapeDtypeStruct((2, width), F32)
    terms = pl.pallas_call(
        functools.partial(weigh_kernel, half_width),
        grid=(1,),
        in_specs=[pl.BlockSpec(memory_space=pltpu.SMEM)] + [whole(x.shape) for x in (*shares, freq_rows)],
        out_specs=[whole(pair.shape)] * 4,
        out_shape=[pair] * 4,
        scratch_shapes=[pltpu.VMEM((5, width), F32)],
        compiler_params=pltpu.CompilerParams(vmem_limit_bytes=4 * 2**20),
    )(place, *shares, freq_rows)
    arrived = [terms[0]] + [swapped(terms[k], k) for k in range(1, 4)]
    carried = (arrived[0] + arrived[1]) + (arrived[2] + arrived[3])
    route = [(b * 4 + s, (b + RETURNS[s]) % modes * 4 + s) for b in range(modes) for s in range(4)]
    result = lax.ppermute(carried[0], ("mode", "atom"), route)
    far = [swapped(result, k) for k in range(1, 4)]
    return factor * (carried[1] + ((result + far[0]) + (far[1] + far[2])))


def solution(mesh):
    return jax.shard_map(
        local,
        mesh=mesh,
        in_specs=(P("atom", "mode"), P(None, None, None, None, "atom"), P(None, "atom"), P()),
        out_specs=P("mode"),
        check_vma=False,
    )
```

```python
import functools
import math

import jax
import jax.numpy as jnp
from jax import lax
from jax.experimental import pallas as pl
from jax.experimental.pallas import tpu as pltpu
from jax.sharding import PartitionSpec as P

HALO = 64
PARTNERS = 4
WIDTH_MODES = 320
BLOCK = 128
WIN = BLOCK + 2 * HALO
ROWS = 3 * BLOCK
HEAD, TAIL = 2, 3
SLOTS = 5
TABLE = 40
F32, BF16 = jnp.float32, jnp.bfloat16


def shifted(x, axis, distance):
    count = lax.axis_size(axis)
    return lax.ppermute(x, axis, [(i, (i + distance) % count) for i in range(count)])


def table_kernel(total_atoms, place_ref, couplings_ref, neighbours_ref, out_ref, rows_ref):
    blocks = neighbours_ref.shape[1] // BLOCK
    lane = lax.broadcasted_iota(jnp.int32, (BLOCK, ROWS), 1)
    atom = lax.broadcasted_iota(jnp.int32, (BLOCK, ROWS), 0)
    spread = jnp.zeros((blocks * TABLE, ROWS), F32)
    for p in range(3):
        for i in range(blocks):
            lanes = slice(i * BLOCK, (i + 1) * BLOCK)
            for k in range(4):
                for a in range(3):
                    at = i * TABLE + (k * 3 + a) * 3
                    rows_ref[at : at + 3, :] = couplings_ref[k, a, p, :, lanes]
            target = neighbours_ref[:, lanes] - ((place_ref[0] * blocks + i) * BLOCK - HALO)
            target = jnp.where(target < 0, target + total_atoms, target)
            target = jnp.where(target >= total_atoms, target - total_atoms, target)
            rows_ref[i * TABLE + 36 : (i + 1) * TABLE, :] = target.astype(F32)
        place = jnp.where(lane == 3 * atom + p, 1.0, 0.0).astype(BF16)
        spread += jnp.dot(rows_ref[...].astype(BF16), place, preferred_element_type=F32)
    for i in range(blocks):
        rows = spread[i * TABLE : (i + 1) * TABLE]
        out_ref[i] = rows
        for k in (0, 2):
            same = rows[36 + k : 37 + k] == rows[37 + k : 38 + k]
            twin = jnp.where(same, rows[(k + 1) * 9 : (k + 2) * 9], 0.0)
            out_ref[i, k * 9 : (k + 1) * 9, :] = rows[k * 9 : (k + 1) * 9] + twin


def operator_table(place, couplings, neighbours, total_atoms):
    blocks = neighbours.shape[1] // BLOCK
    vmem = pl.BlockSpec(memory_space=pltpu.VMEM)
    return pl.pallas_call(
        functools.partial(table_kernel, total_atoms),
        in_specs=[pl.BlockSpec(memory_space=pltpu.SMEM), vmem, vmem],
        out_shape=jax.ShapeDtypeStruct((blocks, TABLE, ROWS), F32),
        scratch_shapes=[pltpu.VMEM((blocks * TABLE, BLOCK), F32)],
        compiler_params=pltpu.CompilerParams(vmem_limit_bytes=16 * 2**20),
        cost_estimate=pl.CostEstimate(flops=2 * 10**9, bytes_accessed=3 * 10**6, transcendentals=0),
    )(place, couplings, neighbours)


TILE = 16


def tile_slots(first_row, first_lane):
    low, high = first_lane // 3 + HALO, (first_lane + 127) // 3 + HALO
    meets = lambda lo, hi: first_row <= hi and lo < first_row + TILE
    up = (0, 1) if meets(low + 2, high + HALO) else ()
    return up + ((2, 3) if meets(low - HALO, high - 2) else ())


def fill_kernel(table_ref, out_ref):
    for block in range(table_ref.shape[0]):
        for first_lane in range(0, ROWS, 128):
            lanes = slice(first_lane, first_lane + 128)
            wide = [
                jnp.broadcast_to(table_ref[block, at : at + 1, lanes], (TILE, 128)).astype(BF16) for at in range(TABLE)
            ]
            for first_row in range(0, WIN, TILE):
                slots = tile_slots(first_row, first_lane)
                row = (lax.broadcasted_iota(jnp.int32, (TILE, 128), 0).astype(F32) + float(first_row)).astype(BF16)
                masks = {k: row == wide[36 + k] for k in slots}
                for a in range(3):
                    for q in range(3):
                        value = jnp.zeros((TILE, 128), BF16)
                        for k in reversed(slots):
                            value = jnp.where(masks[k], wide[(k * 3 + a) * 3 + q], value)
                        start, lane = q * WIN + first_row, a * ROWS + first_lane
                        out_ref[block, start : start + TILE, lane : lane + 128] = value


def filled_operator(table):
    vmem = pl.BlockSpec(memory_space=pltpu.VMEM)
    return pl.pallas_call(
        fill_kernel,
        in_specs=[vmem],
        out_specs=vmem,
        out_shape=jax.ShapeDtypeStruct((table.shape[0], 3 * WIN, 3 * ROWS), BF16),
        compiler_params=pltpu.CompilerParams(vmem_limit_bytes=8 * 2**20),
        cost_estimate=pl.CostEstimate(flops=4 * 10**9, bytes_accessed=10**6, transcendentals=0),
    )(table)


def copy_kernel(moves, *refs):
    for src, s0, dst, d0, n in moves:
        refs[dst][d0 : d0 + n, :] = refs[src][s0 : s0 + n, :]


def copied_rows(inputs, lengths, moves):
    width = inputs[0].shape[1]
    moves = [(i, s, len(inputs) + o, d, n) for i, s, o, d, n in moves]
    return pl.pallas_call(
        functools.partial(copy_kernel, moves),
        out_shape=[jax.ShapeDtypeStruct((n, width), inputs[0].dtype) for n in lengths],
        compiler_params=pltpu.CompilerParams(vmem_limit_bytes=8 * 2**20),
    )(*inputs)


def applied_block(planes_ref, start, operator_ref):
    window = [planes_ref[pl.ds(start + q, WIN, stride=3), :].astype(BF16) for q in range(3)]
    window = jnp.concatenate(window, axis=0).T
    applied = jnp.dot(window, operator_ref[...], preferred_element_type=F32).astype(BF16)
    return jnp.concatenate([applied[:, a * ROWS : (a + 1) * ROWS] for a in range(3)], axis=0)


def add_products(steps, total_ref):
    left = jnp.concatenate([applied for applied, _ in steps], axis=1)
    right = jnp.concatenate([jnp.concatenate(near, axis=1) for _, near in steps], axis=0)
    total_ref[...] += jnp.dot(left, right, preferred_element_type=F32)


def first_kernel(t_ref, far_ref, below_ref, above_ref, p1, own, p2, p3, out_ref, planes):
    tail, edge = TAIL * ROWS, 3 * HALO
    out_ref[...] = jnp.zeros_like(out_ref)
    planes[0:tail, :] = far_ref[0:tail, :].astype(F32)
    planes[tail : tail + edge, :] = above_ref[...].astype(F32)
    planes[tail + edge : tail + 2 * edge, :] = below_ref[...].astype(F32)
    planes[tail + 2 * edge :, :] = far_ref[tail:, :].astype(F32)
    blocks = own.shape[0] // ROWS
    steps = []
    for at in range(ROWS, tail + ROWS, ROWS):
        block = (blocks - TAIL + at // ROWS) % blocks
        near = [r[at : at + ROWS, :] for r in (far_ref, p1, p2, p3)]
        near.insert(2, own[block * ROWS : (block + 1) * ROWS, :])
        steps.append((applied_block(planes, at - edge if block else tail + edge, t_ref.at[block]), near))
    add_products(steps, out_ref)


def second_kernel(
    place_ref, t_ref, before_ref, far_a, far_b, own, a1, a2, a3, b1, b2, b3, o0, o1, o2, o3, planes, total
):
    tail, head = TAIL * ROWS, HEAD * ROWS
    rows_b = far_b.shape[0]
    planes[0:head, :] = far_a[tail:, :].astype(F32)
    planes[head : head + rows_b, :] = far_b[...].astype(F32)
    planes[head + rows_b :, :] = far_a[0:tail, :].astype(F32)
    total[...] = before_ref[...]
    blocks = own.shape[0] // ROWS
    steps = []
    for block in range(1, blocks - TAIL + 1):
        if block < HEAD or block >= blocks - TAIL:
            at = tail + block * ROWS if block < HEAD else (block - blocks + TAIL) * ROWS
            near = [r[at : at + ROWS, :] for r in (far_a, a1, a2, a3)]
        else:
            at = (block - HEAD) * ROWS
            near = [r[at : at + ROWS, :] for r in (far_b, b1, b2, b3)]
        near.insert(2, own[block * ROWS : (block + 1) * ROWS, :])
        steps.append((applied_block(planes, block * ROWS - 3 * HALO, t_ref.at[block]), near))
        if len(steps) == 2 or block == blocks - TAIL:
            add_products(steps, total)
            steps = []
    for k, out in enumerate((o0, o1, o2, o3)):
        share = jnp.bitwise_xor(place_ref[0], k)
        for a in range(3):
            rows = pl.ds(pl.multiple_of(a * 128 + share * 32, 32), 32)
            out[a * 32 : (a + 1) * 32, :] = total[rows, :].astype(BF16)


def star_products(place, operator, own, below, above, firsts, seconds):
    blocks = operator.shape[0]
    width = own.shape[1]
    shape = (3 * width, SLOTS * width)
    vmem = pl.BlockSpec(memory_space=pltpu.VMEM)
    cost = lambda n: pl.CostEstimate(flops=n * 10**9, bytes_accessed=n * 3 * 10**6, transcendentals=0)
    before = pl.pallas_call(
        first_kernel,
        in_specs=[vmem] * 8,
        out_specs=vmem,
        out_shape=jax.ShapeDtypeStruct(shape, F32),
        scratch_shapes=[pltpu.VMEM((firsts[0].shape[0] + 6 * HALO, width), F32)],
        compiler_params=pltpu.CompilerParams(vmem_limit_bytes=10 * 2**20),
        cost_estimate=cost(TAIL),
    )(operator, firsts[0], below, above, firsts[1], own, *firsts[2:])
    steps = blocks - TAIL
    out_shape = (shape[0] // 4, shape[1])
    return pl.pallas_call(
        second_kernel,
        in_specs=[pl.BlockSpec(memory_space=pltpu.SMEM)] + [vmem] * 11,
        out_specs=[vmem] * 4,
        out_shape=[jax.ShapeDtypeStruct(out_shape, BF16)] * 4,
        scratch_shapes=[pltpu.VMEM((blocks * ROWS, width), F32), pltpu.VMEM(shape, F32)],
        compiler_params=pltpu.CompilerParams(vmem_limit_bytes=12 * 2**20),
        cost_estimate=cost(steps),
    )(place, operator, before, firsts[0], seconds[0], own, *firsts[1:], *seconds[1:])


RETURNS = (1, -1, 2, -2)


def weigh_kernel(half_width, place_ref, s0, s1, s2, s3, freq_ref, o0, o1, o2, o3, rows_ref):
    atom, mode = place_ref[0], place_ref[1]
    modes = freq_ref.shape[0]
    summed = s0[...].astype(F32) + s1[...].astype(F32) + s2[...].astype(F32) + s3[...].astype(F32)
    squares = summed[0:32] * summed[0:32] + summed[32:64] * summed[32:64] + summed[64:96] * summed[64:96]
    row = lax.broadcasted_iota(jnp.int32, (32, 128), 0) + 32 * atom
    lane = lax.broadcasted_iota(jnp.int32, (32, 128), 1)
    wrapped = lambda b: jnp.where(b >= modes, b - modes, jnp.where(b < 0, b + modes, b))
    top = wrapped(mode + 2)
    top_freq = freq_ref[pl.ds(top, 1), :]
    centre = jnp.sum(jnp.where(row == lane, top_freq, 0.0), axis=1, keepdims=True)
    own = jnp.zeros((32, 128), F32)
    for slot in range(SLOTS):
        block = wrapped(mode + 2 - slot)
        offset = centre - freq_ref[pl.ds(block, 1), :]
        lorentz = (half_width / math.pi) / (offset * offset + half_width * half_width)
        term = jnp.where(block <= top, squares[:, slot * 128 : (slot + 1) * 128] * lorentz, 0.0)
        own += term
        if slot == 2:
            rows_ref[4:5, :] = jnp.sum(term, axis=0, keepdims=True)
        elif slot > 0:
            at = RETURNS.index(2 - slot)
            rows_ref[at : at + 1, :] = jnp.sum(term, axis=0, keepdims=True)
    own = jnp.sum(own, axis=1, keepdims=True)
    at = RETURNS.index(2)
    rows_ref[at : at + 1, :] = jnp.sum(jnp.where(row == lane, own, 0.0), axis=0, keepdims=True)
    for k, out in enumerate((o0, o1, o2, o3)):
        out[0:1, :] = rows_ref[pl.ds(jnp.bitwise_xor(atom, k), 1), :]
        out[1:2, :] = rows_ref[4:5, :]


def swapped(x, k):
    return lax.ppermute(x, "atom", [(i, i ^ k) for i in range(4)])


def local(vectors, couplings, neighbours, frequency):
    rows_dev, width = vectors.shape
    atoms_dev = rows_dev // 3
    atom_groups = lax.axis_size("atom")
    modes = lax.axis_size("mode")
    half_width = WIDTH_MODES / (width * modes)
    place = jnp.stack([lax.axis_index("atom"), lax.axis_index("mode")]).astype(jnp.int32)
    edge = 3 * HALO
    head, tail = HEAD * ROWS, TAIL * ROWS
    rest = rows_dev - head - tail
    own_a, own_b = copied_rows(
        [vectors],
        [head + tail, rest],
        [(0, rows_dev - tail, 0, 0, tail), (0, 0, 0, tail, head), (0, head, 1, 0, rest)],
    )
    up1a = shifted(own_a, "mode", -1)
    dn1a = shifted(own_a, "mode", 1)
    up1b = shifted(own_b, "mode", -1)
    dn1b = shifted(own_b, "mode", 1)
    operator = operator_table(place, couplings, neighbours, atoms_dev * atom_groups)
    up1a, dn1a, operator = lax.optimization_barrier((up1a, dn1a, operator))
    up2a = shifted(up1a, "mode", -1)
    dn2a = shifted(dn1a, "mode", 1)
    up2b = shifted(up1b, "mode", -1)
    dn2b = shifted(dn1b, "mode", 1)
    below = shifted(up2a[tail - edge : tail], "atom", 1)
    above = shifted(up2a[tail : tail + edge], "atom", -1)

    operator, up2a = lax.optimization_barrier((operator, up2a))
    operator = filled_operator(operator)
    shares = star_products(
        place, operator, vectors, below, above, [up2a, up1a, dn1a, dn2a], [up2b, up1b, dn1b, dn2b]
    )
    shares = [shares[0]] + [swapped(shares[k], k) for k in range(1, 4)]

    own_freq = lax.dynamic_slice_in_dim(frequency, place[1] * width, width)
    factor, seconds_done = lax.optimization_barrier((math.pi / (3.0 * own_freq * own_freq), shares[0]))
    shares[0] = seconds_done
    whole = lambda shape: pl.BlockSpec(shape, lambda g: (0, 0))
    freq_rows = frequency.reshape(modes, width)
    pair = jax.ShapeDtypeStruct((2, width), F32)
    terms = pl.pallas_call(
        functools.partial(weigh_kernel, half_width),
        grid=(1,),
        in_specs=[pl.BlockSpec(memory_space=pltpu.SMEM)] + [whole(x.shape) for x in (*shares, freq_rows)],
        out_specs=[whole(pair.shape)] * 4,
        out_shape=[pair] * 4,
        scratch_shapes=[pltpu.VMEM((5, width), F32)],
        compiler_params=pltpu.CompilerParams(vmem_limit_bytes=4 * 2**20),
    )(place, *shares, freq_rows)
    arrived = [terms[0]] + [swapped(terms[k], k) for k in range(1, 4)]
    carried = (arrived[0] + arrived[1]) + (arrived[2] + arrived[3])
    route = [(b * 4 + s, (b + RETURNS[s]) % modes * 4 + s) for b in range(modes) for s in range(4)]
    result = lax.ppermute(carried[0], ("mode", "atom"), route)
    far = [swapped(result, k) for k in range(1, 4)]
    return factor * (carried[1] + ((result + far[0]) + (far[1] + far[2])))


def solution(mesh):
    return jax.shard_map(
        local,
        mesh=mesh,
        in_specs=(P("atom", "mode"), P(None, None, None, None, "atom"), P(None, "atom"), P()),
        out_specs=P("mode"),
        check_vma=False,
    )
```
